128 devices in a mesh: sec: 2 (over x_lo), head: 8 (over z, x_hi), seq: 8 (over y, core).
Axes of the slice: x: 4 (x_hi: 2, x_lo: 2; x = x_hi * 2 + x_lo), y: 4, z: 4, core: 2. Of those that a mesh axis runs over, the one named last changes fastest.
Arguments:
- inputs: bfloat16 [8, 2048, 4096], P('seq', 'sec'), may hold values from -16 to 16
- w_query: bfloat16 [4096, 4096], P(None, 'head'), may hold values from -0.09375 to 0.09375
- w_key: bfloat16 [4096, 1024], P(None, 'head'), may hold values from -0.09375 to 0.09375
- teacher_queries: bfloat16 [8, 2048, 16384], P('seq', 'head', 'sec'), may hold values from -256 to 256
- teacher_keys: bfloat16 [8, 2048, 16384], P('seq', 'head', 'sec'), may hold values from -8 to 8
- head_match: int32 [32], replicated, may hold values from 0 to 127, as said below
- block_order: int32 [16], replicated, may hold values from 0 to 15, each once
Outputs:
- grad_inputs: bfloat16 [8, 2048, 4096], P('seq', ('sec', 'head'))
- grad_query: bfloat16 [4096, 4096], P(('sec', 'seq'), 'head')
- grad_key: bfloat16 [4096, 1024], P(('sec', 'seq'), 'head')
The draws below stay inside these ranges and needn't reach their ends.
Inputs may be any that keep to these rules, and one draw needn't show every extreme that they name: `head_match`: entries may repeat. Split the teacher heads into 2 aligned sections of 64: heads s * 64 to (s + 1) * 64 - 1. Within each aligned block of 4 entries starting at entry 0, at most 2 distinct teacher heads lie in each aligned section, and some run of entries has exactly 2 distinct ones in section 0. `block_order`: each block index once.
All inputs are finite; a program needn't handle non-finite values.
Results may differ from the reference program's by a relative error of at most 0.025.
Values may be sent and summed in bfloat16 or wider, within the bound.
A program may use at most 128 MiB of HBM per device.

```python
import math
import jax
import jax.numpy as jnp
from jax import lax

D = 4096
SH = 32
KVH = 8
HD = 128
TH = 128
SEQ_LEN = 2048
QB = 128
SEQS = 8
NBLK = 16
HEADS_DEV = 4
TH_SEC = 64
CAPACITY = 2
N_SEC = 2
N_HEAD = 8


def draw_inputs(key, part):
    key = jax.random.fold_in(key, 3)
    first_key = jax.random.fold_in(key, 0)
    shape = (SEQS, SEQ_LEN, D)
    values = jnp.clip(jax.random.normal(first_key, shape, jnp.float32), -6.0, 6.0)
    return values.astype(jnp.bfloat16)


def teacher_pair(key):
    keys = jax.random.split(key, 2)
    shape = (SEQS, SEQ_LEN, TH, HD)
    queries = jnp.clip(jax.random.normal(keys[0], shape, jnp.float32), -6.0, 6.0)
    keys_part = jnp.clip(jax.random.normal(keys[1], shape, jnp.float32), -6.0, 6.0)
    flat = (SEQS, SEQ_LEN, TH * HD)
    return (queries.reshape(flat), keys_part.reshape(flat))


def draw_teacher_queries(key, part):
    queries, keys_part = teacher_pair(key)
    return queries.astype(jnp.bfloat16)


def draw_teacher_keys(key, part):
    queries, keys_part = teacher_pair(key)
    return keys_part.astype(jnp.bfloat16)


def draw_head_match(key, part):
    key = jax.random.fold_in(key, 7)
    groups = SH // HEADS_DEV
    sections_count = TH // TH_SEC
    keys = jax.random.split(key, 6)
    counts = jax.random.randint(keys[0], (groups, sections_count), 1, CAPACITY + 1)
    special = jax.random.randint(keys[1], (), 0, groups)
    forced = (jnp.arange(groups)[:, None] == special) & (jnp.arange(sections_count)[None, :] == 0)
    counts = jnp.where(forced, CAPACITY, counts)
    picks = jax.vmap(lambda sub: jax.random.permutation(sub, TH_SEC)[:CAPACITY])(jax.random.split(keys[2], groups * sections_count))
    picks = picks.reshape(groups, sections_count * CAPACITY)
    sections = jax.random.randint(keys[3], (groups, HEADS_DEV), 0, sections_count)
    drawn = jax.random.randint(keys[4], (groups, HEADS_DEV), 0, 1 << 20)
    slot_place = jnp.arange(HEADS_DEV)[None, :]
    is_special = (jnp.arange(groups) == special)[:, None] & (slot_place < CAPACITY)
    sections = jnp.where(is_special, 0, sections)
    chosen_count = jnp.take_along_axis(counts, sections, axis=1)
    which = jnp.where(is_special, slot_place, drawn % chosen_count)
    heads = sections * TH_SEC + jnp.take_along_axis(picks, sections * CAPACITY + which, axis=1)
    shuffle = jax.vmap(lambda sub: jax.random.permutation(sub, HEADS_DEV))(jax.random.split(keys[5], groups))
    heads = jnp.take_along_axis(heads, shuffle, axis=1)
    return heads.reshape(SH).astype(jnp.int32)


def level_of(stream_key, shape, cuts, low, high):
    def one(axis_at, blocks):
        draws = jax.random.uniform(jax.random.fold_in(jax.random.fold_in(stream_key, 6), axis_at), (blocks,), jnp.float32, low / len(cuts), high / len(cuts))
        return jnp.repeat(jnp.exp(draws), shape[axis_at] // blocks).reshape((-1,) + (1,) * (len(shape) - axis_at - 1))

    gain = one(*cuts[0])
    for cut in cuts[1:]:
        gain = gain * one(*cut)
    return gain


def normal_values(key, extent, deviation, bound, cuts=(), kind=jnp.bfloat16):
    level = level_of(key, extent, cuts, -0.22, 0.18) if cuts else 1.0
    values = jax.random.normal(key, extent, jnp.float32) * deviation * level
    return jnp.minimum(jnp.maximum(values, -bound), bound).astype(kind)


def setup_inputs(seed: int = 0) -> dict:
    splits = jax.random.split(jax.random.key(seed), 8)
    return {
        "inputs": draw_inputs(jax.random.fold_in(splits[7], 71), 0),
        "w_query": normal_values(splits[1], (D, SH * HD), D ** -0.5, 0.09375, ((1, 8),)),
        "w_key": normal_values(splits[2], (D, KVH * HD), D ** -0.5, 0.09375, ((1, 8),)),
        "teacher_queries": draw_teacher_queries(jax.random.fold_in(splits[7], 71), 0),
        "teacher_keys": draw_teacher_keys(jax.random.fold_in(splits[7], 71), 0),
        "head_match": draw_head_match(jax.random.fold_in(splits[7], 71), 0),
        "block_order": jax.random.permutation(splits[6], NBLK).astype(jnp.int32),
    }


rope_base = 500000.0
grad_scale = 16.0

def positions_of(block_order):
    offsets = jnp.arange(QB, dtype=jnp.int32)
    return (block_order[:, None] * QB + offsets[None, :]).reshape(-1).astype(jnp.int32)

def rope_tables(positions):
    half = HD // 2
    freqs = rope_base ** (-(jnp.arange(half, dtype=jnp.float32) * 2.0) / HD)
    angles = positions.astype(jnp.float32)[:, None] * freqs[None, :]
    return (jnp.cos(angles), jnp.sin(angles))

def rotate(values, cosine, sine):
    half = values.shape[-1] // 2
    first = values[..., :half]
    second = values[..., half:]
    return jnp.concatenate([first * cosine - second * sine, second * cosine + first * sine], axis=-1)

def rotate_back(grads, cosine, sine):
    half = grads.shape[-1] // 2
    first = grads[..., :half]
    second = grads[..., half:]
    return jnp.concatenate([first * cosine + second * sine, second * cosine - first * sine], axis=-1)

def masked_softmax(scores, visible):
    masked = jnp.where(visible, scores, -jnp.inf)
    top = lax.optimization_barrier(jnp.max(masked, axis=-1, keepdims=True))
    weights = jnp.where(visible, jnp.exp(masked - top), 0.0)
    return weights / lax.optimization_barrier(jnp.sum(weights, axis=-1, keepdims=True))

def reference(inputs, w_query, w_key, teacher_queries, teacher_keys, head_match, block_order):
    scale = 1.0 / math.sqrt(HD)
    group = SH // KVH
    positions = positions_of(block_order)
    visible = positions[None, :] <= positions[:, None]
    cosine, sine = rope_tables(positions)
    rows = SEQ_LEN // N_SEC
    query_cols = SH * HD // N_HEAD
    key_cols = KVH * HD // N_HEAD

    def one_sequence(carry, seq_data):
        query_total, key_total = carry
        tokens, t_queries, t_keys = seq_data
        queries = jnp.dot(tokens, w_query, preferred_element_type=jnp.float32).reshape(SEQ_LEN, SH, HD).transpose(1, 0, 2)
        queries = rotate(queries, cosine, sine).astype(jnp.bfloat16)
        keys = jnp.dot(tokens, w_key, preferred_element_type=jnp.float32).reshape(SEQ_LEN, KVH, HD).transpose(1, 0, 2)
        keys = rotate(keys, cosine, sine).astype(jnp.bfloat16)
        chosen_q = t_queries.reshape(SEQ_LEN, TH, HD)[:, head_match].transpose(1, 0, 2)
        chosen_k = t_keys.reshape(SEQ_LEN, TH, HD)[:, head_match].transpose(1, 0, 2)

        def one_group(kv_group):
            query4 = lax.dynamic_slice_in_dim(queries, kv_group * group, group, 0).astype(jnp.float32)
            key_one = lax.dynamic_index_in_dim(keys, kv_group, 0, keepdims=False).astype(jnp.float32)
            teach_q = lax.dynamic_slice_in_dim(chosen_q, kv_group * group, group, 0).astype(jnp.float32)
            teach_k = lax.dynamic_slice_in_dim(chosen_k, kv_group * group, group, 0).astype(jnp.float32)
            student = jnp.einsum('hqd,kd->hqk', query4, key_one) * scale
            teacher = jnp.einsum('hqd,hkd->hqk', teach_q, teach_k) * scale
            p_student = masked_softmax(student, visible)
            p_teacher = masked_softmax(teacher, visible)
            score_grads = ((p_student - p_teacher) * grad_scale).astype(jnp.bfloat16).astype(jnp.float32)
            query_grads = jnp.einsum('hqk,kd->hqd', score_grads, key_one) * scale
            query_grads = rotate_back(query_grads, cosine, sine).astype(jnp.bfloat16)
            key_grads = jnp.einsum('hqk,hqd->kd', score_grads, query4) * scale
            key_grads = rotate_back(key_grads, cosine, sine).astype(jnp.bfloat16)
            return (query_grads, key_grads)
        query_parts, key_parts = lax.map(one_group, jnp.arange(KVH, dtype=jnp.int32))
        grad_queries = query_parts.reshape(SH, SEQ_LEN, HD).transpose(1, 0, 2).reshape(SEQ_LEN, SH * HD)
        grad_keys = key_parts.transpose(1, 0, 2).reshape(SEQ_LEN, KVH * HD)
        total = jnp.zeros((SEQ_LEN, D), jnp.float32)
        for part in range(N_HEAD):
            q_block = grad_queries[:, part * query_cols:(part + 1) * query_cols]
            k_block = grad_keys[:, part * key_cols:(part + 1) * key_cols]
            term = jnp.dot(q_block, w_query[:, part * query_cols:(part + 1) * query_cols].T, preferred_element_type=jnp.float32)
            term = term + jnp.dot(k_block, w_key[:, part * key_cols:(part + 1) * key_cols].T, preferred_element_type=jnp.float32)
            total = total + lax.optimization_barrier(term.astype(jnp.bfloat16)).astype(jnp.float32)
        for half in range(N_SEC):
            token_rows = tokens[half * rows:(half + 1) * rows]
            term_q = jnp.dot(token_rows.T, grad_queries[half * rows:(half + 1) * rows], preferred_element_type=jnp.float32)
            term_k = jnp.dot(token_rows.T, grad_keys[half * rows:(half + 1) * rows], preferred_element_type=jnp.float32)
            query_total = query_total + lax.optimization_barrier(term_q.astype(jnp.bfloat16)).astype(jnp.float32)
            key_total = key_total + lax.optimization_barrier(term_k.astype(jnp.bfloat16)).astype(jnp.float32)
        return ((query_total, key_total), total.astype(jnp.bfloat16))
    start = (jnp.zeros((D, SH * HD), jnp.float32), jnp.zeros((D, KVH * HD), jnp.float32))
    (query_total, key_total), grad_inputs = lax.scan(one_sequence, start, (inputs, teacher_queries, teacher_keys))
    return (grad_inputs, query_total.astype(jnp.bfloat16), key_total.astype(jnp.bfloat16))
```

```python
import math

import jax
import jax.numpy as jnp
from jax import lax
from jax.experimental import pallas as pl
from jax.experimental.pallas import tpu as pltpu
from jax.sharding import PartitionSpec as P

HD = 128
QB = 128
NBLK = 16
HALF_BLKS = 8
HEADS = 4
TH_SEC = 64
GROUPS = 8
ROWS = 1024
LEN = 2048
TROWS = 256
D = 4096
GW = 640
QW = 512
CK = 256
MIB = 1024 * 1024

rope_base = 500000.0
grad_scale = 16.0
scale = 1.0 / math.sqrt(HD)
MESH = pl.DeviceIdType.MESH
ANY = pl.BlockSpec(memory_space=pl.ANY)
VMEM = pl.BlockSpec(memory_space=pltpu.VMEM)
SMEM = pl.BlockSpec(memory_space=pltpu.SMEM)
DMA = pltpu.SemaphoreType.DMA
F32 = jnp.float32
BF16 = jnp.bfloat16


def rope_rows(block_order, sec):
    own = lax.dynamic_slice_in_dim(block_order, sec * HALF_BLKS, HALF_BLKS, 0)
    positions = (own[:, None] * QB + jnp.arange(QB, dtype=jnp.int32)[None, :]).reshape(-1)
    half = HD // 2
    freqs = rope_base ** (-(jnp.arange(half, dtype=F32) * 2.0) / HD)
    angles = positions.astype(F32)[:, None] * freqs[None, :]
    cosine, sine = jnp.cos(angles), jnp.sin(angles)
    return jnp.stack(
        [
            jnp.concatenate([cosine, cosine], axis=1),
            jnp.concatenate([-sine, sine], axis=1),
        ]
    )


def section_slots(match_ref, group, section):
    low, high = jnp.int32(TH_SEC - 1), jnp.int32(0)
    for i in range(HEADS):
        local = match_ref[group * HEADS + i] - section * TH_SEC
        inside = (local >= 0) & (local < TH_SEC)
        low = jnp.minimum(low, jnp.where(inside, local, TH_SEC - 1))
        high = jnp.maximum(high, jnp.where(inside, local, 0))
    return low, high


def pick_kernel(match_ref, tk_ref, tq_ref, k_out, q_out, k_v, q_v, in_sems, out_sems):
    sec = lax.axis_index("sec")
    copies = []
    for g in range(GROUPS):
        for j, local in enumerate(section_slots(match_ref, g, sec)):
            columns = pl.ds(pl.multiple_of(local * HD, HD), HD)
            for a, (src, held, dst) in enumerate(((tk_ref, k_v, k_out), (tq_ref, q_v, q_out))):
                place = held.at[g // 2, g % 2, j]
                load = pltpu.make_async_copy(src.at[0, :, columns], place, in_sems.at[a, g * 2 + j])
                load.start()
                store = pltpu.make_async_copy(
                    place, dst.at[g // 2, g % 2, j], out_sems.at[a, g * 2 + j]
                )
                copies.append((load, store))
    for load, store in copies:
        load.wait()
        store.start()
    for load, store in copies:
        store.wait()


def pick(match, teacher_keys, teacher_queries):
    shape = (4, 2, 2, TROWS, HD)
    return pl.pallas_call(
        pick_kernel,
        out_shape=(jax.ShapeDtypeStruct(shape, BF16), jax.ShapeDtypeStruct(shape, BF16)),
        in_specs=[SMEM, ANY, ANY],
        out_specs=(ANY, ANY),
        scratch_shapes=[
            pltpu.VMEM(shape, BF16),
            pltpu.VMEM(shape, BF16),
            DMA((2, 16)),
            DMA((2, 16)),
        ],
        name="pick",
    )(match, teacher_keys, teacher_queries)


def spread_kernel(
    sk, sq, tok, wq, wk, rope,
    q_out, keys_out, gotk, gotq, w2,
    rope_v, tok_v, w_v, k_v, zk, zq,
    load_sem, own_sem, zs, zr, pks, pkr, cks, ckr, rks, rkr, qps, qpr, qxs, qxr,
    keys_s, keys_r, w1s, w1r, wys, wyr, wrs, wrr, wcs, wcr,
):
    sec, head, seq = lax.axis_index("sec"), lax.axis_index("head"), lax.axis_index("seq")
    z, xh = head // 2, head % 2
    y, c = seq // 2, seq % 2
    partner = {"sec": 1 - sec}
    cross = {"sec": 1 - sec, "head": z * 2 + 1 - xh}
    far = {"head": z * 2 + 1 - xh}
    core = {"seq": y * 2 + 1 - c}
    up = {"seq": ((y + 1) % 4) * 2 + c}
    down = {"seq": ((y + 3) % 4) * 2 + c}

    def depth(d):
        return {"head": ((z + d) % 4) * 2 + xh}

    def send(src, dst, ss, rs, where):
        return pltpu.make_async_remote_copy(
            src_ref=src, dst_ref=dst, send_sem=ss, recv_sem=rs, device_id=where, device_id_type=MESH
        )

    loads = [
        pltpu.make_async_copy(wq, w_v.at[:, pl.ds(0, QW)], load_sem.at[4]),
        pltpu.make_async_copy(wk, w_v.at[:, pl.ds(QW, HD)], load_sem.at[5]),
        pltpu.make_async_copy(rope, rope_v, load_sem.at[6]),
    ]
    for load in loads:
        load.start()

    def token_load(r):
        rows = pl.ds(pl.multiple_of(r * 256, 256), 256)
        return pltpu.make_async_copy(tok.at[0, rows], tok_v.at[rows], load_sem.at[r])

    for r in range(4):
        token_load(r).start()

    barrier = pltpu.get_barrier_semaphore()
    greet = [partner, cross, far, core, up, down, depth(1), depth(2), depth(3)]
    for where in greet:
        pl.semaphore_signal(barrier, inc=1, device_id=where, device_id_type=MESH)
    pl.semaphore_wait(barrier, len(greet))

    zcopies = []
    for d in (1, 3, 2):
        to = (z + d) % 4
        for a, (src, dst) in enumerate(((sk, zk), (sq, zq))):
            copy = send(src.at[to], dst.at[d - 1], zs.at[a, d - 1], zr.at[a, d - 1], depth(d))
            copy.start()
            zcopies.append(copy)

    def krows(d, xhs):
        return pl.ds(pl.multiple_of((((z + 4 - d) % 4) * 2 + xhs) * TROWS, TROWS), TROWS)

    def qrows(d, xhs):
        return pl.ds(
            pl.multiple_of(((((z + 4 - d) % 4) * 2 + xhs) % 4) * TROWS, TROWS), TROWS
        )

    def held(d):
        return (sk.at[z], sq.at[z]) if d == 0 else (zk.at[d - 1], zq.at[d - 1])

    def along_x(d):
        kd, qd = held(d)
        half = ((z + 4 - d) % 4) // 2
        mine = gotk.at[sec, :, krows(d, xh)]
        mine_q = gotq.at[sec, :, qrows(d, xh)]
        return dict(
            ck=send(kd.at[1 - xh], mine, cks.at[d], ckr.at[d], cross),
            pk=send(kd.at[xh], mine, pks.at[d], pkr.at[d], partner),
            qx=send(
                qd.at[1 - xh], mine_q, qxs.at[d], qxr.at[d, sec],
                {"sec": half, "head": z * 2 + 1 - xh},
            ),
            qp=send(qd.at[xh], mine_q, qps.at[d], qpr.at[d], partner),
            lk=pltpu.make_async_copy(kd.at[xh], mine, own_sem.at[0, d]),
            lq=pltpu.make_async_copy(qd.at[xh], mine_q, own_sem.at[1, d]),
            half=half,
        )

    def start_x(d):
        m = along_x(d)
        m["ck"].start()
        m["pk"].start()
        m["qx"].start()

        @pl.when(m["half"] != sec)
        def _():
            m["qp"].start()

        m["lk"].start()

        @pl.when(m["half"] == sec)
        def _():
            m["lq"].start()

    def relay(d):
        got = gotk.at[1 - sec, :, krows(d, 1 - xh)]
        return send(got, got, rks.at[d], rkr.at[d], partner)

    start_x(0)

    for load in loads:
        load.wait()

    def piece(ref, yy, cc, j):
        start = ((yy % 4) * 2 + cc) * 512 + j * 256
        return ref.at[pl.ds(pl.multiple_of(start, 256), 256)]

    first = []
    for j in range(2):
        copy = send(piece(w_v, y, c, j), piece(w2, y, c, j), w1s.at[j], w1r.at[j], cross)
        copy.start()
        first.append(copy)

    def project(r, _):
        token_load(r).wait()
        rows = pl.ds(pl.multiple_of(r * 256, 256), 256)
        product = jnp.dot(tok_v[rows, :], w_v[...], preferred_element_type=F32)
        cosine, sine = rope_v[0, rows, :], rope_v[1, rows, :]
        for h in range(HEADS + 1):
            part = product[:, h * HD : (h + 1) * HD]
            part = (part * cosine + pltpu.roll(part, HD // 2, axis=1) * sine).astype(BF16)
            if h < HEADS:
                q_out[rows, h * HD : (h + 1) * HD] = part
            else:
                k_v[rows, :] = part
        return 0

    lax.fori_loop(0, 4, project, 0)
    key_rows = keys_out.at[pl.ds(pl.multiple_of(sec * ROWS, ROWS), ROWS)]
    key_send = send(k_v, key_rows, keys_s, keys_r, partner)
    key_send.start()
    key_own = pltpu.make_async_copy(k_v, key_rows, own_sem.at[2, 0])
    key_own.start()

    relays = []

    def wait_relay(d):
        got = gotk.at[1 - sec, :, krows(d, 1 - xh)]
        send(got, got, cks.at[d], ckr.at[d], cross).wait_recv()
        copy = relay(d)
        copy.start()
        relays.append(copy)

    wait_relay(0)
    for d in (1, 3):
        zcopies[0 if d == 1 else 2].wait_recv()
        zcopies[1 if d == 1 else 3].wait_recv()
        start_x(d)

    wcopies = []

    def forward(src_y, j, sems, rsems, index, where):
        ref = piece(w2, src_y, c, j)
        copy = send(ref, ref, sems.at[index], rsems.at[index], where)
        copy.start()
        wcopies.append(copy)

    def wait_piece(src_y, cc, j, sem, rsem):
        ref = piece(w2, src_y, cc, j)
        send(ref, ref, sem, rsem, core).wait_recv()

    for j in range(2):
        wait_piece(y, c, j, w1s.at[j], w1r.at[j])
        forward(y, j, wys, wyr, j, up)
        forward(y, j, wys, wyr, 2 + j, down)
        forward(y, j, wcs, wcr, j, core)
    wait_relay(1)
    wait_relay(3)
    zcopies[4].wait_recv()
    zcopies[5].wait_recv()
    start_x(2)
    wait_piece(y + 3, c, 0, wys.at[0], wyr.at[0])
    forward(y + 3, 0, wrs, wrr, 0, up)
    forward(y + 3, 0, wcs, wcr, 2, core)
    wait_piece(y + 1, c, 1, wys.at[3], wyr.at[3])
    forward(y + 1, 1, wrs, wrr, 1, down)
    forward(y + 1, 1, wcs, wcr, 3, core)
    wait_relay(2)
    wait_piece(y + 3, c, 1, wys.at[1], wyr.at[1])
    forward(y + 3, 1, wcs, wcr, 4, core)
    wait_piece(y + 1, c, 0, wys.at[2], wyr.at[2])
    forward(y + 1, 0, wcs, wcr, 5, core)
    wait_piece(y + 2, c, 0, wrs.at[0], wrr.at[0])
    forward(y + 2, 0, wcs, wcr, 6, core)
    wait_piece(y + 2, c, 1, wrs.at[1], wrr.at[1])
    forward(y + 2, 1, wcs, wcr, 7, core)

    for index, (dy, j) in enumerate(((0, 0), (0, 1), (3, 0), (1, 1), (3, 1), (1, 0), (2, 0), (2, 1))):
        wait_piece(y + dy, 1 - c, j, wcs.at[index], wcr.at[index])
    other_rows = keys_out.at[pl.ds(pl.multiple_of((1 - sec) * ROWS, ROWS), ROWS)]
    send(k_v, other_rows, keys_s, keys_r, partner).wait_recv()
    for d in range(4):
        m = along_x(d)
        got = gotk.at[1 - sec, :, krows(d, xh)]
        send(got, got, pks.at[d], pkr.at[d], partner).wait_recv()
        got = gotk.at[sec, :, krows(d, 1 - xh)]
        send(got, got, rks.at[d], rkr.at[d], partner).wait_recv()

        @pl.when(m["half"] == sec)
        def _():
            got = gotq.at[1 - sec, :, qrows(d, xh)]
            send(got, got, qps.at[d], qpr.at[d], partner).wait_recv()
            for source in range(2):
                got = gotq.at[source, :, qrows(d, 1 - xh)]
                send(got, got, qxs.at[d], qxr.at[d, source], cross).wait_recv()
            m["lq"].wait()

        @pl.when(m["half"] != sec)
        def _():
            m["qp"].wait_send()

        m["lk"].wait()
        m["ck"].wait_send()
        m["pk"].wait_send()
        m["qx"].wait_send()
    key_own.wait()
    key_send.wait_send()
    for copy in zcopies + first + relays + wcopies:
        copy.wait_send()


def spread(picked_k, picked_q, inputs, w_query, w_key, rope):
    return pl.pallas_call(
        spread_kernel,
        out_shape=(
            jax.ShapeDtypeStruct((ROWS, QW), BF16),
            jax.ShapeDtypeStruct((LEN, HD), BF16),
            jax.ShapeDtypeStruct((2, 2, LEN, HD), BF16),
            jax.ShapeDtypeStruct((2, 2, ROWS, HD), BF16),
            jax.ShapeDtypeStruct((D, GW), BF16),
        ),
        in_specs=[ANY] * 6,
        out_specs=(VMEM, ANY, ANY, ANY, ANY),
        scratch_shapes=[
            pltpu.VMEM((2, ROWS, HD), F32),
            pltpu.VMEM((ROWS, D), BF16),
            pltpu.VMEM((D, GW), BF16),
            pltpu.VMEM((ROWS, HD), BF16),
            pltpu.VMEM((3, 2, 2, TROWS, HD), BF16),
            pltpu.VMEM((3, 2, 2, TROWS, HD), BF16),
            DMA((7,)),
            DMA((3, 4)),
            DMA((2, 3)), DMA((2, 3)),
            DMA((4,)), DMA((4,)),
            DMA((4,)), DMA((4,)),
            DMA((4,)), DMA((4,)),
            DMA((4,)), DMA((4,)),
            DMA((4,)), DMA((4, 2)),
            DMA, DMA,
            DMA((2,)), DMA((2,)),
            DMA((4,)), DMA((4,)),
            DMA((2,)), DMA((2,)),
            DMA((8,)), DMA((8,)),
        ],
        compiler_params=pltpu.CompilerParams(
            collective_id=1, has_side_effects=True, vmem_limit_bytes=48 * MIB
        ),
        name="spread",
    )(picked_k, picked_q, inputs, w_query, w_key, rope)


def attend_kernel(
    order_ref, match_ref, q_ref, keys, gotq, gotk, rope,
    qg_ref, own_ref, other_ref,
    kp, tkp, tqv, st, g_acc, dk, sems, qsems,
):
    sec, head = lax.axis_index("sec"), lax.axis_index("head")
    exponent = scale * math.log2(math.e)
    lows = [section_slots(match_ref, head, section)[0] for section in range(2)]
    places = []
    for i in range(HEADS):
        entry = match_ref[head * HEADS + i]
        section = entry // TH_SEC
        low = jnp.where(section == 0, lows[0], lows[1])
        slot = jnp.where(entry - section * TH_SEC == low, 0, 1)
        places.append((section, slot))
    copies = []
    for i, (section, slot) in enumerate(places):
        copies.append(pltpu.make_async_copy(gotq.at[section, slot], tqv.at[i], qsems.at[i]))
        copies[-1].start()
    for b in range(NBLK):
        to = pl.ds(pl.multiple_of(order_ref[b] * QB, QB), QB)
        at = pl.ds(b * QB, QB)
        copies.append(pltpu.make_async_copy(keys.at[at], kp.at[to], sems.at[4, b]))
        copies[-1].start()
        for i, (section, slot) in enumerate(places):
            copies.append(
                pltpu.make_async_copy(gotk.at[section, slot, at], tkp.at[i, to], sems.at[i, b])
            )
            copies[-1].start()
    dk[...] = jnp.zeros_like(dk)
    for copy in copies:
        copy.wait()

    nt = (((1,), (1,)), ((), ()))
    tn = (((0,), (0,)), ((), ()))

    def one_block(qb, _):
        rows = pl.ds(pl.multiple_of(qb * QB, QB), QB)
        block = order_ref[sec * HALF_BLKS + qb]
        last = block // 2
        queries = jnp.concatenate(
            [q_ref[rows, i * HD : (i + 1) * HD] for i in range(HEADS)], axis=0
        )

        def scores(chunk, top, masked):
            at = pl.ds(pl.multiple_of(chunk * CK, CK), CK)
            student = lax.dot_general(kp[at, :], queries, nt, preferred_element_type=F32)
            teacher = jnp.concatenate(
                [
                    lax.dot_general(tkp[i, at, :], tqv[i, rows, :], nt, preferred_element_type=F32)
                    for i in range(HEADS)
                ],
                axis=1,
            )
            both = jnp.concatenate([student, teacher], axis=1)
            if masked:
                key_at = lax.broadcasted_iota(jnp.int32, both.shape, 0) + chunk * CK
                row_at = lax.broadcasted_iota(jnp.int32, both.shape, 1) % QB + block * QB
                both = jnp.where(key_at <= row_at, both, -jnp.inf)
            st[at, :] = both
            return jnp.maximum(top, jnp.max(both.reshape(CK // 8, 8, 2 * QW), axis=0))

        top = jnp.full((8, 2 * QW), -jnp.inf, F32)
        top = lax.fori_loop(0, last, lambda chunk, t: scores(chunk, t, False), top)
        top = scores(last, top, True)
        top = jnp.max(top, axis=0, keepdims=True)

        def weights(chunk, total):
            at = pl.ds(pl.multiple_of(chunk * CK, CK), CK)
            e = jnp.exp2((st[at, :] - top) * exponent)
            st[at, :] = e
            return total + jnp.sum(e.reshape(CK // 8, 8, 2 * QW), axis=0)

        total = lax.fori_loop(0, last + 1, weights, jnp.zeros((8, 2 * QW), F32))
        inverse = grad_scale / jnp.sum(total, axis=0, keepdims=True)
        g_acc[...] = jnp.zeros_like(g_acc)

        def grads(chunk, _):
            at = pl.ds(pl.multiple_of(chunk * CK, CK), CK)
            g = (st[at, :QW] * inverse[:, :QW] - st[at, QW:] * inverse[:, QW:]).astype(BF16)
            dk[at, :] += jnp.dot(g, queries, preferred_element_type=F32)
            g_acc[...] += lax.dot_general(g, kp[at, :], tn, preferred_element_type=F32)
            return 0

        lax.fori_loop(0, last + 1, grads, 0)
        cosine, sine = rope[0, rows, :], rope[1, rows, :]
        for i in range(HEADS):
            part = g_acc[i * QB : (i + 1) * QB, :] * scale
            part = part * cosine - pltpu.roll(part, HD // 2, axis=1) * sine
            qg_ref[rows, i * HD : (i + 1) * HD] = part.astype(BF16)
        return 0

    lax.fori_loop(0, HALF_BLKS, one_block, 0)
    for b in range(HALF_BLKS):
        at = pl.ds(b * QB, QB)
        for half, ref in ((sec, own_ref), (1 - sec, other_ref)):
            block = order_ref[half * HALF_BLKS + b]
            part = dk[pl.ds(pl.multiple_of(block * QB, QB), QB), :] * scale
            ref[at, :] = part.astype(ref.dtype)


def attend(order, match, queries, keys, gotq, gotk, rope):
    return pl.pallas_call(
        attend_kernel,
        out_shape=(
            jax.ShapeDtypeStruct((ROWS, QW), BF16),
            jax.ShapeDtypeStruct((ROWS, HD), F32),
            jax.ShapeDtypeStruct((ROWS, HD), BF16),
        ),
        in_specs=[SMEM, SMEM, VMEM, ANY, ANY, ANY, VMEM],
        out_specs=(VMEM, VMEM, VMEM),
        scratch_shapes=[
            pltpu.VMEM((LEN, HD), BF16),
            pltpu.VMEM((HEADS, LEN, HD), BF16),
            pltpu.VMEM((HEADS, ROWS, HD), BF16),
            pltpu.VMEM((LEN, 2 * QW), F32),
            pltpu.VMEM((QW, HD), F32),
            pltpu.VMEM((LEN, HD), F32),
            DMA((HEADS + 1, NBLK)),
            DMA((HEADS,)),
        ],
        compiler_params=pltpu.CompilerParams(vmem_limit_bytes=48 * MIB),
        name="attend",
    )(order, match, queries, keys, gotq, gotk, rope)


def finish_kernel(
    qg, own, other, tok, wq, wk, w2, rope,
    rows_out, gq_out, gk_out,
    own_v, rope_v,
    tok_v, w_v, w2_v, gt, gk_v, key_rx, g2, k2, z_tx, z_rx, c_tx, c_rx, y_tx, y_rx, s_tx, s_rx, qg_v,
    load_sem, key_s, key_r, x_s, x_r, zs, zr, cs, cr, ys, yr, ss, sr,
):
    sec, head, seq = lax.axis_index("sec"), lax.axis_index("head"), lax.axis_index("seq")
    z, xh = head // 2, head % 2
    y, c = seq // 2, seq % 2
    partner = {"sec": 1 - sec}
    far = {"head": z * 2 + 1 - xh}
    core = {"seq": y * 2 + 1 - c}
    around_y = ({"seq": ((y + 1) % 4) * 2 + c}, {"seq": ((y + 3) % 4) * 2 + c})
    around_z = ({"head": ((z + 1) % 4) * 2 + xh}, {"head": ((z + 3) % 4) * 2 + xh})

    def send(src, dst, ss_, rs_, where):
        return pltpu.make_async_remote_copy(
            src_ref=src, dst_ref=dst, send_sem=ss_, recv_sem=rs_, device_id=where, device_id_type=MESH
        )

    loads = [
        pltpu.make_async_copy(qg, qg_v, load_sem.at[0]),
        pltpu.make_async_copy(tok.at[0], tok_v, load_sem.at[1]),
        pltpu.make_async_copy(wq, w_v.at[:, pl.ds(0, QW)], load_sem.at[2]),
        pltpu.make_async_copy(wk, w_v.at[:, pl.ds(QW, HD)], load_sem.at[3]),
        pltpu.make_async_copy(w2, w2_v, load_sem.at[4]),
    ]
    small = [
        pltpu.make_async_copy(own, own_v, load_sem.at[5]),
        pltpu.make_async_copy(rope, rope_v, load_sem.at[6]),
    ]
    for load in loads[:1] + small + loads[1:]:
        load.start()

    barrier = pltpu.get_barrier_semaphore()
    greet = [partner, far, core, *around_y, *around_z]
    for where in greet:
        pl.semaphore_signal(barrier, inc=1, device_id=where, device_id_type=MESH)
    pl.semaphore_wait(barrier, len(greet))

    key_send = send(other, key_rx, key_s, key_r, partner)
    key_send.start()
    q_send = send(qg.at[:, 1 - xh], g2, x_s.at[0], x_r.at[0], far)
    q_send.start()
    loads[0].wait()
    for b in range(HALF_BLKS):
        gt[0:QW, b * QB : (b + 1) * QB] = qg_v[b // 2, b % 2].T
    for load in small:
        load.wait()
    key_send.wait_recv()
    for b in range(HALF_BLKS):
        at = pl.ds(b * QB, QB)
        total = own_v[at, :] + key_rx[at, :].astype(F32)
        total = total * rope_v[0, at, :] - pltpu.roll(total, HD // 2, axis=1) * rope_v[1, at, :]
        total = total.astype(BF16)
        gk_v[b // 2, b % 2] = total
        gt[QW:GW, b * QB : (b + 1) * QB] = total.T
    k_send = send(gk_v.at[:, 1 - xh], k2, x_s.at[1], x_r.at[1], far)
    k_send.start()

    def weight_part(s, yy, cc):
        start = (s * 8 + (yy % 4) * 2 + cc) * 256
        return jnp.dot(
            gt[...], tok_v[:, pl.ds(pl.multiple_of(start, 256), 256)], preferred_element_type=F32
        )

    def core_copy(i):
        return send(c_tx.at[i], c_rx.at[i], cs.at[i], cr.at[i], core)

    loads[1].wait()

    def to_core(i, _):
        s, step = i % 2, i // 2
        yy = jnp.where(s == 0, y + 3 - step, y + 1 + step) % 4
        c_tx[i] = weight_part(s, yy, 1 - c).astype(BF16)
        core_copy(i).start()
        return 0

    lax.fori_loop(0, 8, to_core, 0)
    for load in loads[2:]:
        load.wait()
    q_send.wait_recv()
    k_send.wait_recv()

    nt = (((1,), (1,)), ((), ()))

    def row_term(zz, column):
        at = pl.ds(column, 1024)
        zz = zz % 4
        own = jnp.concatenate([qg_v[zz, xh], gk_v[zz, xh]], axis=1)
        theirs = jnp.concatenate([g2[zz], k2[zz]], axis=1)
        return lax.dot_general(
            own, w_v[at, :], nt, preferred_element_type=F32
        ) + lax.dot_general(theirs, w2_v[at, :], nt, preferred_element_type=F32)

    def z_copy(stream, step):
        return send(
            z_tx.at[stream, step], z_rx.at[stream, step],
            zs.at[stream, step], zr.at[stream, step], around_z[stream // 2],
        )

    def z_step(step):
        for stream in (0, 2, 1, 3):
            target = z + 3 - step if stream < 2 else z + 1 + step
            term = row_term(target, stream * 1024)
            if step > 0:
                z_copy(stream, step - 1).wait_recv()
                term = term + z_rx[stream, step - 1].astype(F32)
            if step < 3:
                z_tx[stream, step] = term.astype(BF16)
                z_copy(stream, step).start()
            else:
                rows_out[:, stream * 1024 : (stream + 1) * 1024] = term.astype(BF16)

    def y_copy(stream, step):
        return send(
            y_tx.at[stream, step], y_rx.at[stream, step],
            ys.at[stream, step], yr.at[stream, step], around_y[stream],
        )

    def y_total(stream, step):
        target = y + 3 - step if stream == 0 else y + 1 + step
        total = weight_part(stream, target, c)
        core_copy(step * 2 + stream).wait_recv()
        total = total + c_rx[step * 2 + stream].astype(F32)
        if step > 0:
            y_copy(stream, step - 1).wait_recv()
            total = total + y_rx[stream, step - 1].astype(F32)
        return total

    def y_step(step):
        for stream in range(2):
            y_tx[stream, step] = y_total(stream, step).astype(BF16)
            y_copy(stream, step).start()

    z_step(0)
    y_step(0)
    z_step(1)
    y_step(1)
    y_step(2)
    z_step(2)
    sec_copy = send(s_tx, s_rx, ss, sr, partner)
    first, second = y_total(0, 3), y_total(1, 3)
    keep = jnp.where(sec == 0, first, second)
    s_tx[...] = jnp.where(sec == 0, second, first).astype(BF16)
    sec_copy.start()
    z_step(3)
    sec_copy.wait_recv()
    keep = (keep + s_rx[...].astype(F32)).T
    gq_out[...] = keep[:, :QW].astype(BF16)
    gk_out[...] = keep[:, QW:].astype(BF16)

    for copy in (key_send, q_send, k_send, sec_copy):
        copy.wait_send()
    for i in range(8):
        core_copy(i).wait_send()
    for step in range(3):
        for stream in range(4):
            z_copy(stream, step).wait_send()
        for stream in range(2):
            y_copy(stream, step).wait_send()


def finish(qg, own, other, inputs, w_query, w_key, w2, rope):
    return pl.pallas_call(
        finish_kernel,
        out_shape=(
            jax.ShapeDtypeStruct((QB, D), BF16),
            jax.ShapeDtypeStruct((256, QW), BF16),
            jax.ShapeDtypeStruct((256, HD), BF16),
        ),
        in_specs=[ANY] * 8,
        out_specs=(VMEM, VMEM, VMEM),
        scratch_shapes=[
            pltpu.VMEM((ROWS, HD), F32),
            pltpu.VMEM((2, ROWS, HD), F32),
            pltpu.VMEM((ROWS, D), BF16),
            pltpu.VMEM((D, GW), BF16),
            pltpu.VMEM((D, GW), BF16),
            pltpu.VMEM((GW, ROWS), BF16),
            pltpu.VMEM((4, 2, QB, HD), BF16),
            pltpu.VMEM((ROWS, HD), BF16),
            pltpu.VMEM((4, QB, QW), BF16),
            pltpu.VMEM((4, QB, HD), BF16),
            pltpu.VMEM((4, 3, QB, 1024), BF16),
            pltpu.VMEM((4, 3, QB, 1024), BF16),
            pltpu.VMEM((8, GW, 256), BF16),
            pltpu.VMEM((8, GW, 256), BF16),
            pltpu.VMEM((2, 3, GW, 256), BF16),
            pltpu.VMEM((2, 3, GW, 256), BF16),
            pltpu.VMEM((GW, 256), BF16),
            pltpu.VMEM((GW, 256), BF16),
            pltpu.VMEM((4, 2, QB, QW), BF16),
            DMA((7,)),
            DMA, DMA,
            DMA((2,)), DMA((2,)),
            DMA((4, 3)), DMA((4, 3)),
            DMA((8,)), DMA((8,)),
            DMA((2, 3)), DMA((2, 3)),
            DMA, DMA,
        ],
        compiler_params=pltpu.CompilerParams(
            collective_id=2, has_side_effects=True, vmem_limit_bytes=58 * MIB
        ),
        name="finish",
    )(qg, own, other, inputs, w_query, w_key, w2, rope)


def shards(inputs, w_query, w_key, teacher_queries, teacher_keys, head_match, block_order):
    rope = rope_rows(block_order, lax.axis_index("sec"))
    picked_k, picked_q = pick(head_match, teacher_keys, teacher_queries)
    queries, keys, gotk, gotq, w2 = spread(picked_k, picked_q, inputs, w_query, w_key, rope)
    query_grads, own, other = attend(block_order, head_match, queries, keys, gotq, gotk, rope)
    rows, grad_query, grad_key = finish(
        query_grads.reshape(4, 2, QB, QW), own, other, inputs, w_query, w_key, w2, rope
    )
    return (rows[None], grad_query, grad_key)


def solution(mesh):
    return jax.shard_map(
        shards,
        mesh=mesh,
        in_specs=(
            P("seq", "sec", None),
            P(None, "head"),
            P(None, "head"),
            P("seq", "head", "sec"),
            P("seq", "head", "sec"),
            P(),
            P(),
        ),
        out_specs=(
            P("seq", ("sec", "head"), None),
            P(("sec", "seq"), "head"),
            P(("sec", "seq"), "head"),
        ),
        check_vma=False,
    )
```

```python
import math

import jax
import jax.numpy as jnp
from jax import lax
from jax.experimental import pallas as pl
from jax.experimental.pallas import tpu as pltpu
from jax.sharding import PartitionSpec as P

HD = 128
QB = 128
NBLK = 16
HALF_BLKS = 8
HEADS = 4
TH_SEC = 64
GROUPS = 8
ROWS = 1024
LEN = 2048
TROWS = 256
D = 4096
GW = 640
QW = 512
CK = 256
MIB = 1024 * 1024
LOWEST = -1e30

rope_base = 500000.0
grad_scale = 16.0
scale = 1.0 / math.sqrt(HD)
MESH = pl.DeviceIdType.MESH
ANY = pl.BlockSpec(memory_space=pl.ANY)
VMEM = pl.BlockSpec(memory_space=pltpu.VMEM)
SMEM = pl.BlockSpec(memory_space=pltpu.SMEM)
DMA = pltpu.SemaphoreType.DMA
F32 = jnp.float32
BF16 = jnp.bfloat16


def section_slots(match_ref, group, section):
    low, high = jnp.int32(TH_SEC - 1), jnp.int32(0)
    for i in range(HEADS):
        local = match_ref[group * HEADS + i] - section * TH_SEC
        inside = (local >= 0) & (local < TH_SEC)
        low = jnp.minimum(low, jnp.where(inside, local, TH_SEC - 1))
        high = jnp.maximum(high, jnp.where(inside, local, 0))
    return low, high


def pick_kernel(
    match_ref, order_ref, freqs, tk_ref, tq_ref, k_out, q_out, rope, k_v, q_v, in_sems, out_sems
):
    sec = lax.axis_index("sec")
    copies = []
    for g in range(GROUPS):
        for j, local in enumerate(section_slots(match_ref, g, sec)):
            columns = pl.ds(pl.multiple_of(local * HD, HD), HD)
            for a, (src, held, dst) in enumerate(((tk_ref, k_v, k_out), (tq_ref, q_v, q_out))):
                place = held.at[g // 2, g % 2, j]
                load = pltpu.make_async_copy(src.at[0, :, columns], place, in_sems.at[a, g * 2 + j])
                load.start()
                store = pltpu.make_async_copy(
                    place, dst.at[g // 2, g % 2, j], out_sems.at[a, g * 2 + j]
                )
                copies.append((load, store))
    lane = lax.broadcasted_iota(jnp.int32, (QB, HD), 1)
    offset = lax.broadcasted_iota(jnp.int32, (QB, HD), 0)

    def one_block(b, _):
        position = order_ref[sec * HALF_BLKS + b] * QB + offset
        angles = position.astype(F32) * freqs[...]
        at = pl.ds(pl.multiple_of(b * QB, QB), QB)
        sine = jnp.sin(angles)
        rope[0, at, :] = jnp.cos(angles)
        rope[1, at, :] = jnp.where(lane < HD // 2, -sine, sine)
        return 0

    lax.fori_loop(0, HALF_BLKS, one_block, 0)
    for load, store in copies:
        load.wait()
        store.start()
    for load, store in copies:
        store.wait()


def pick(match, order, teacher_keys, teacher_queries):
    half = HD // 2
    freqs = rope_base ** (-(jnp.arange(half, dtype=F32) * 2.0) / HD)
    freqs = jnp.concatenate([freqs, freqs])[None]
    shape = (4, 2, 2, TROWS, HD)
    return pl.pallas_call(
        pick_kernel,
        out_shape=(
            jax.ShapeDtypeStruct(shape, BF16),
            jax.ShapeDtypeStruct(shape, BF16),
            jax.ShapeDtypeStruct((2, ROWS, HD), F32),
        ),
        in_specs=[SMEM, SMEM, VMEM, ANY, ANY],
        out_specs=(ANY, ANY, VMEM),
        scratch_shapes=[
            pltpu.VMEM(shape, BF16),
            pltpu.VMEM(shape, BF16),
            DMA((2, 16)),
            DMA((2, 16)),
        ],
        compiler_params=pltpu.CompilerParams(vmem_limit_bytes=63 * MIB),
        name="pick",
    )(match, order, freqs, teacher_keys, teacher_queries)


def spread_kernel(
    sk, sq, tok, wq, wk, rope,
    q_out, keys_out, gotk, gotq, w2,
    rope_v, tok_v, w_v, k_v, zk, zq,
    load_sem, own_sem, zs, zr, pks, pkr, cks, ckr, rks, rkr, qps, qpr, qxs, qxr,
    keys_s, keys_r, w1s, w1r, wys, wyr, wrs, wrr, wcs, wcr,
):
    sec, head, seq = lax.axis_index("sec"), lax.axis_index("head"), lax.axis_index("seq")
    z, xh = head // 2, head % 2
    y, c = seq // 2, seq % 2
    partner = {"sec": 1 - sec}
    cross = {"sec": 1 - sec, "head": z * 2 + 1 - xh}
    far = {"head": z * 2 + 1 - xh}
    core = {"seq": y * 2 + 1 - c}
    up = {"seq": ((y + 1) % 4) * 2 + c}
    down = {"seq": ((y + 3) % 4) * 2 + c}

    def depth(d):
        return {"head": ((z + d) % 4) * 2 + xh}

    def send(src, dst, ss, rs, where):
        return pltpu.make_async_remote_copy(
            src_ref=src, dst_ref=dst, send_sem=ss, recv_sem=rs, device_id=where, device_id_type=MESH
        )

    loads = [
        pltpu.make_async_copy(wq, w_v.at[:, pl.ds(0, QW)], load_sem.at[4]),
        pltpu.make_async_copy(wk, w_v.at[:, pl.ds(QW, HD)], load_sem.at[5]),
        pltpu.make_async_copy(rope, rope_v, load_sem.at[6]),
    ]
    for load in loads:
        load.start()

    def token_load(r):
        rows = pl.ds(pl.multiple_of(r * 256, 256), 256)
        return pltpu.make_async_copy(tok.at[0, rows], tok_v.at[rows], load_sem.at[r])

    for r in range(4):
        token_load(r).start()

    barrier = pltpu.get_barrier_semaphore()
    greet = [partner, cross, far, core, up, down, depth(1), depth(2), depth(3)]
    for where in greet:
        pl.semaphore_signal(barrier, inc=1, device_id=where, device_id_type=MESH)
    pl.semaphore_wait(barrier, len(greet))

    def along_z(a, d):
        src, dst = ((sk, zk), (sq, zq))[a]
        return send(
            src.at[(z + d) % 4], dst.at[d - 1], zs.at[a, d - 1], zr.at[a, d - 1], depth(d)
        )

    for d in (1, 3, 2):
        along_z(0, d).start()

    def krows(d, xhs):
        return pl.ds(pl.multiple_of((((z + 4 - d) % 4) * 2 + xhs) * TROWS, TROWS), TROWS)

    def qrows(d, xhs):
        return pl.ds(
            pl.multiple_of(((((z + 4 - d) % 4) * 2 + xhs) % 4) * TROWS, TROWS), TROWS
        )

    def held(d):
        return (sk.at[z], sq.at[z]) if d == 0 else (zk.at[d - 1], zq.at[d - 1])

    def along_x(d):
        kd, qd = held(d)
        half = ((z + 4 - d) % 4) // 2
        mine = gotk.at[sec, :, krows(d, xh)]
        mine_q = gotq.at[sec, :, qrows(d, xh)]
        return dict(
            ck=send(kd.at[1 - xh], mine, cks.at[d], ckr.at[d], cross),
            pk=send(kd.at[xh], mine, pks.at[d], pkr.at[d], partner),
            qx=send(
                qd.at[1 - xh], mine_q, qxs.at[d], qxr.at[d, sec],
                {"sec": half, "head": z * 2 + 1 - xh},
            ),
            qp=send(qd.at[xh], mine_q, qps.at[d], qpr.at[d], partner),
            lk=pltpu.make_async_copy(kd.at[xh], mine, own_sem.at[0, d]),
            lq=pltpu.make_async_copy(qd.at[xh], mine_q, own_sem.at[1, d]),
            half=half,
        )

    def start_keys(d):
        m = along_x(d)
        m["ck"].start()
        m["pk"].start()
        m["lk"].start()

    def start_queries(d):
        m = along_x(d)
        m["qx"].start()

        @pl.when(m["half"] != sec)
        def _():
            m["qp"].start()

        @pl.when(m["half"] == sec)
        def _():
            m["lq"].start()

    def relay(d):
        got = gotk.at[1 - sec, :, krows(d, 1 - xh)]
        return send(got, got, rks.at[d], rkr.at[d], partner)

    start_keys(0)
    start_queries(0)

    for load in loads:
        load.wait()

    def piece(ref, yy, cc, j):
        start = ((yy % 4) * 2 + cc) * 512 + j * 256
        return ref.at[pl.ds(pl.multiple_of(start, 256), 256)]

    first = []
    for j in range(2):
        copy = send(piece(w_v, y, c, j), piece(w2, y, c, j), w1s.at[j], w1r.at[j], cross)
        copy.start()
        first.append(copy)

    def project(r, _):
        token_load(r).wait()
        rows = pl.ds(pl.multiple_of(r * 256, 256), 256)
        product = jnp.dot(tok_v[rows, :], w_v[...], preferred_element_type=F32)
        cosine, sine = rope_v[0, rows, :], rope_v[1, rows, :]
        for h in range(HEADS + 1):
            part = product[:, h * HD : (h + 1) * HD]
            part = (part * cosine + pltpu.roll(part, HD // 2, axis=1) * sine).astype(BF16)
            if h < HEADS:
                q_out[rows, h * HD : (h + 1) * HD] = part
            else:
                k_v[rows, :] = part
        return 0

    lax.fori_loop(0, 4, project, 0)
    key_rows = keys_out.at[pl.ds(pl.multiple_of(sec * ROWS, ROWS), ROWS)]
    key_send = send(k_v, key_rows, keys_s, keys_r, partner)
    key_send.start()
    key_own = pltpu.make_async_copy(k_v, key_rows, own_sem.at[2, 0])
    key_own.start()

    relays = []

    def wait_relay(d):
        got = gotk.at[1 - sec, :, krows(d, 1 - xh)]
        send(got, got, cks.at[d], ckr.at[d], cross).wait_recv()
        copy = relay(d)
        copy.start()
        relays.append(copy)

    for d in (1, 3, 2):
        along_z(1, d).start()
    wait_relay(0)
    for d in (1, 3):
        along_z(0, d).wait_recv()
        start_keys(d)

    wcopies = []

    def forward(src_y, j, sems, rsems, index, where):
        ref = piece(w2, src_y, c, j)
        copy = send(ref, ref, sems.at[index], rsems.at[index], where)
        copy.start()
        wcopies.append(copy)

    def wait_piece(src_y, cc, j, sem, rsem):
        ref = piece(w2, src_y, cc, j)
        send(ref, ref, sem, rsem, core).wait_recv()

    for j in range(2):
        wait_piece(y, c, j, w1s.at[j], w1r.at[j])
        forward(y, j, wys, wyr, j, up)
        forward(y, j, wys, wyr, 2 + j, down)
        forward(y, j, wcs, wcr, j, core)
    wait_relay(1)
    wait_relay(3)
    along_z(0, 2).wait_recv()
    start_keys(2)
    for d in (1, 3):
        along_z(1, d).wait_recv()
        start_queries(d)
    wait_piece(y + 3, c, 0, wys.at[0], wyr.at[0])
    forward(y + 3, 0, wrs, wrr, 0, up)
    forward(y + 3, 0, wcs, wcr, 2, core)
    wait_piece(y + 1, c, 1, wys.at[3], wyr.at[3])
    forward(y + 1, 1, wrs, wrr, 1, down)
    forward(y + 1, 1, wcs, wcr, 3, core)
    wait_relay(2)
    along_z(1, 2).wait_recv()
    start_queries(2)
    wait_piece(y + 3, c, 1, wys.at[1], wyr.at[1])
    forward(y + 3, 1, wcs, wcr, 4, core)
    wait_piece(y + 1, c, 0, wys.at[2], wyr.at[2])
    forward(y + 1, 0, wcs, wcr, 5, core)
    wait_piece(y + 2, c, 0, wrs.at[0], wrr.at[0])
    forward(y + 2, 0, wcs, wcr, 6, core)
    wait_piece(y + 2, c, 1, wrs.at[1], wrr.at[1])
    forward(y + 2, 1, wcs, wcr, 7, core)

    for index, (dy, j) in enumerate(((0, 0), (0, 1), (3, 0), (1, 1), (3, 1), (1, 0), (2, 0), (2, 1))):
        wait_piece(y + dy, 1 - c, j, wcs.at[index], wcr.at[index])
    other_rows = keys_out.at[pl.ds(pl.multiple_of((1 - sec) * ROWS, ROWS), ROWS)]
    send(k_v, other_rows, keys_s, keys_r, partner).wait_recv()
    for d in range(4):
        m = along_x(d)
        got = gotk.at[1 - sec, :, krows(d, xh)]
        send(got, got, pks.at[d], pkr.at[d], partner).wait_recv()
        got = gotk.at[sec, :, krows(d, 1 - xh)]
        send(got, got, rks.at[d], rkr.at[d], partner).wait_recv()

        @pl.when(m["half"] == sec)
        def _():
            got = gotq.at[1 - sec, :, qrows(d, xh)]
            send(got, got, qps.at[d], qpr.at[d], partner).wait_recv()
            for source in range(2):
                got = gotq.at[source, :, qrows(d, 1 - xh)]
                send(got, got, qxs.at[d], qxr.at[d, source], cross).wait_recv()
            m["lq"].wait()

        @pl.when(m["half"] != sec)
        def _():
            m["qp"].wait_send()

        m["lk"].wait()
        m["ck"].wait_send()
        m["pk"].wait_send()
        m["qx"].wait_send()
    key_own.wait()
    key_send.wait_send()
    for d in (1, 3, 2):
        for a in range(2):
            along_z(a, d).wait_send()
    for copy in first + relays + wcopies:
        copy.wait_send()


def spread(picked_k, picked_q, inputs, w_query, w_key, rope):
    return pl.pallas_call(
        spread_kernel,
        out_shape=(
            jax.ShapeDtypeStruct((ROWS, QW), BF16),
            jax.ShapeDtypeStruct((LEN, HD), BF16),
            jax.ShapeDtypeStruct((2, 2, LEN, HD), BF16),
            jax.ShapeDtypeStruct((2, 2, ROWS, HD), BF16),
            jax.ShapeDtypeStruct((D, GW), BF16),
        ),
        in_specs=[ANY] * 6,
        out_specs=(VMEM, ANY, ANY, ANY, ANY),
        scratch_shapes=[
            pltpu.VMEM((2, ROWS, HD), F32),
            pltpu.VMEM((ROWS, D), BF16),
            pltpu.VMEM((D, GW), BF16),
            pltpu.VMEM((ROWS, HD), BF16),
            pltpu.VMEM((3, 2, 2, TROWS, HD), BF16),
            pltpu.VMEM((3, 2, 2, TROWS, HD), BF16),
            DMA((7,)),
            DMA((3, 4)),
            DMA((2, 3)), DMA((2, 3)),
            DMA((4,)), DMA((4,)),
            DMA((4,)), DMA((4,)),
            DMA((4,)), DMA((4,)),
            DMA((4,)), DMA((4,)),
            DMA((4,)), DMA((4, 2)),
            DMA, DMA,
            DMA((2,)), DMA((2,)),
            DMA((4,)), DMA((4,)),
            DMA((2,)), DMA((2,)),
            DMA((8,)), DMA((8,)),
        ],
        compiler_params=pltpu.CompilerParams(
            collective_id=1, has_side_effects=True, vmem_limit_bytes=63 * MIB
        ),
        name="spread",
    )(picked_k, picked_q, inputs, w_query, w_key, rope)


def attend_kernel(
    order_ref, match_ref, q_ref, keys, gotq, gotk, rope,
    qg_ref, own_ref, other_ref,
    kp, tkp, tqv, st, ms, g_acc, dk, sems, qsems,
):
    sec, head = lax.axis_index("sec"), lax.axis_index("head")
    exponent = scale * math.log2(math.e)
    lows = [section_slots(match_ref, head, section)[0] for section in range(2)]
    places = []
    for i in range(HEADS):
        entry = match_ref[head * HEADS + i]
        section = entry // TH_SEC
        low = jnp.where(section == 0, lows[0], lows[1])
        slot = jnp.where(entry - section * TH_SEC == low, 0, 1)
        places.append((section, slot))
    copies = []
    for i, (section, slot) in enumerate(places):
        copies.append(pltpu.make_async_copy(gotq.at[section, slot], tqv.at[i], qsems.at[i]))
        copies[-1].start()
    for b in range(NBLK):
        to = pl.ds(pl.multiple_of(order_ref[b] * QB, QB), QB)
        at = pl.ds(b * QB, QB)
        copies.append(pltpu.make_async_copy(keys.at[at], kp.at[to], sems.at[4, b]))
        copies[-1].start()
        for i, (section, slot) in enumerate(places):
            copies.append(
                pltpu.make_async_copy(gotk.at[section, slot, at], tkp.at[i, to], sems.at[i, b])
            )
            copies[-1].start()
    dk[...] = jnp.zeros_like(dk)
    for copy in copies:
        copy.wait()

    nt = (((1,), (1,)), ((), ()))
    tn = (((0,), (0,)), ((), ()))

    def one_block(qb, _):
        rows = pl.ds(pl.multiple_of(qb * QB, QB), QB)
        block = order_ref[sec * HALF_BLKS + qb]
        last = block // 2
        queries = jnp.concatenate(
            [q_ref[rows, i * HD : (i + 1) * HD] for i in range(HEADS)], axis=0
        )

        def scores(chunk, carry, masked):
            at = pl.ds(pl.multiple_of(chunk * CK, CK), CK)
            tops, totals = [], []
            for unit in range(6):
                if unit < 2:
                    columns = slice(unit * 256, unit * 256 + 256)
                    part = lax.dot_general(
                        kp[at, :], queries[columns], nt, preferred_element_type=F32
                    )
                else:
                    i = unit - 2
                    columns = slice(QW + i * HD, QW + (i + 1) * HD)
                    part = lax.dot_general(
                        tkp[i, at, :], tqv[i, rows, :], nt, preferred_element_type=F32
                    )
                if masked:
                    key_at = lax.broadcasted_iota(jnp.int32, part.shape, 0) + chunk * CK
                    row_at = lax.broadcasted_iota(jnp.int32, part.shape, 1) % QB + block * QB
                    part = jnp.where(key_at <= row_at, part, LOWEST)
                part = part.reshape(CK // 8, 8, part.shape[1])
                before, total = carry[0][:, columns], carry[1][:, columns]
                top = jnp.maximum(before, jnp.max(part, axis=0))
                part = jnp.exp2((part - top[None]) * exponent)
                st[at, columns] = part.reshape(CK, part.shape[2])
                tops.append(top)
                totals.append(total * jnp.exp2((before - top) * exponent) + jnp.sum(part, axis=0))
            tops, totals = jnp.concatenate(tops, axis=1), jnp.concatenate(totals, axis=1)
            ms[chunk] = tops
            return tops, totals

        carry = (jnp.full((8, 2 * QW), LOWEST, F32), jnp.zeros((8, 2 * QW), F32))
        carry = lax.fori_loop(0, last, lambda chunk, t: scores(chunk, t, False), carry)
        tops, totals = scores(last, carry, True)
        top = jnp.max(tops, axis=0, keepdims=True)
        totals = totals * jnp.exp2((tops - top) * exponent)
        inverse = grad_scale / jnp.sum(totals, axis=0, keepdims=True)
        g_acc[...] = jnp.zeros_like(g_acc)

        def grads(chunk, _):
            at = pl.ds(pl.multiple_of(chunk * CK, CK), CK)
            factor = jnp.exp2((ms[chunk] - top) * exponent) * inverse
            both = st[at, :].reshape(CK // 8, 8, 2 * QW)
            g = both[:, :, :QW] * factor[None, :, :QW] - both[:, :, QW:] * factor[None, :, QW:]
            g = g.reshape(CK, QW).astype(BF16)
            dk[at, :] += jnp.dot(g, queries, preferred_element_type=F32)
            g_acc[...] += lax.dot_general(g, kp[at, :], tn, preferred_element_type=F32)
            return 0

        lax.fori_loop(0, last + 1, grads, 0)
        cosine, sine = rope[0, rows, :], rope[1, rows, :]
        for i in range(HEADS):
            part = g_acc[i * QB : (i + 1) * QB, :] * scale
            part = part * cosine - pltpu.roll(part, HD // 2, axis=1) * sine
            qg_ref[rows, i * HD : (i + 1) * HD] = part.astype(BF16)
        return 0

    lax.fori_loop(0, HALF_BLKS, one_block, 0)
    for b in range(HALF_BLKS):
        at = pl.ds(b * QB, QB)
        for half, ref in ((sec, own_ref), (1 - sec, other_ref)):
            block = order_ref[half * HALF_BLKS + b]
            part = dk[pl.ds(pl.multiple_of(block * QB, QB), QB), :] * scale
            ref[at, :] = part.astype(ref.dtype)


def attend(order, match, queries, keys, gotq, gotk, rope):
    return pl.pallas_call(
        attend_kernel,
        out_shape=(
            jax.ShapeDtypeStruct((ROWS, QW), BF16),
            jax.ShapeDtypeStruct((ROWS, HD), F32),
            jax.ShapeDtypeStruct((ROWS, HD), BF16),
        ),
        in_specs=[SMEM, SMEM, VMEM, ANY, ANY, ANY, VMEM],
        out_specs=(VMEM, VMEM, VMEM),
        scratch_shapes=[
            pltpu.VMEM((LEN, HD), BF16),
            pltpu.VMEM((HEADS, LEN, HD), BF16),
            pltpu.VMEM((HEADS, ROWS, HD), BF16),
            pltpu.VMEM((LEN, 2 * QW), F32),
            pltpu.VMEM((LEN // CK, 8, 2 * QW), F32),
            pltpu.VMEM((QW, HD), F32),
            pltpu.VMEM((LEN, HD), F32),
            DMA((HEADS + 1, NBLK)),
            DMA((HEADS,)),
        ],
        compiler_params=pltpu.CompilerParams(vmem_limit_bytes=63 * MIB),
        name="attend",
    )(order, match, queries, keys, gotq, gotk, rope)


def finish_kernel(
    qg, own, other, tok, wq, wk, w2, rope,
    rows_out, gq_out, gk_out,
    own_v, rope_v,
    tok_v, w_v, w2_v, gt, gk_v, key_rx, g2, k2, z_tx, z_rx, c_tx, c_rx, y_tx, y_rx, s_tx, s_rx, qg_v,
    load_sem, key_s, key_r, x_s, x_r, zs, zr, cs, cr, ys, yr, ss, sr,
):
    sec, head, seq = lax.axis_index("sec"), lax.axis_index("head"), lax.axis_index("seq")
    z, xh = head // 2, head % 2
    y, c = seq // 2, seq % 2
    partner = {"sec": 1 - sec}
    far = {"head": z * 2 + 1 - xh}
    core = {"seq": y * 2 + 1 - c}
    around_y = ({"seq": ((y + 1) % 4) * 2 + c}, {"seq": ((y + 3) % 4) * 2 + c})
    around_z = ({"head": ((z + 1) % 4) * 2 + xh}, {"head": ((z + 3) % 4) * 2 + xh})

    def send(src, dst, ss_, rs_, where):
        return pltpu.make_async_remote_copy(
            src_ref=src, dst_ref=dst, send_sem=ss_, recv_sem=rs_, device_id=where, device_id_type=MESH
        )

    loads = [
        pltpu.make_async_copy(qg, qg_v, load_sem.at[0]),
        pltpu.make_async_copy(tok.at[0], tok_v, load_sem.at[1]),
        pltpu.make_async_copy(wq, w_v.at[:, pl.ds(0, QW)], load_sem.at[2]),
        pltpu.make_async_copy(wk, w_v.at[:, pl.ds(QW, HD)], load_sem.at[3]),
        pltpu.make_async_copy(w2, w2_v, load_sem.at[4]),
    ]
    small = [
        pltpu.make_async_copy(own, own_v, load_sem.at[5]),
        pltpu.make_async_copy(rope, rope_v, load_sem.at[6]),
    ]
    for load in loads[:1] + small + loads[1:]:
        load.start()

    barrier = pltpu.get_barrier_semaphore()
    greet = [partner, far, core, *around_y, *around_z]
    for where in greet:
        pl.semaphore_signal(barrier, inc=1, device_id=where, device_id_type=MESH)
    pl.semaphore_wait(barrier, len(greet))

    key_send = send(other, key_rx, key_s, key_r, partner)
    key_send.start()

    def far_copy(a, r):
        zz = (z + r) % 4
        src, dst = ((qg, g2), (gk_v, k2))[a]
        return send(src.at[zz, 1 - xh], dst.at[zz], x_s.at[a, r], x_r.at[a, r], far)

    for r in (3, 1):
        far_copy(0, r).start()
    loads[0].wait()
    for b in range(HALF_BLKS):
        gt[0:QW, b * QB : (b + 1) * QB] = qg_v[b // 2, b % 2].T
    for load in small:
        load.wait()
    key_send.wait_recv()
    for b in range(HALF_BLKS):
        at = pl.ds(b * QB, QB)
        total = own_v[at, :] + key_rx[at, :].astype(F32)
        total = total * rope_v[0, at, :] - pltpu.roll(total, HD // 2, axis=1) * rope_v[1, at, :]
        total = total.astype(BF16)
        gk_v[b // 2, b % 2] = total
        gt[QW:GW, b * QB : (b + 1) * QB] = total.T
    for r in (3, 1, 2, 0):
        far_copy(1, r).start()
    for r in (2, 0):
        far_copy(0, r).start()

    def weight_part(s, yy, cc):
        start = (s * 8 + (yy % 4) * 2 + cc) * 256
        return jnp.dot(
            gt[...], tok_v[:, pl.ds(pl.multiple_of(start, 256), 256)], preferred_element_type=F32
        )

    def core_copy(i):
        return send(c_tx.at[i], c_rx.at[i], cs.at[i], cr.at[i], core)

    loads[1].wait()

    def to_core(i, _):
        s, step = i % 2, i // 2
        yy = jnp.where(s == 0, y + 3 - step, y + 1 + step) % 4
        c_tx[i] = weight_part(s, yy, 1 - c).astype(BF16)
        core_copy(i).start()
        return 0

    lax.fori_loop(0, 8, to_core, 0)
    for load in loads[2:]:
        load.wait()

    nt = (((1,), (1,)), ((), ()))

    def row_term(zz, column):
        at = pl.ds(column, 1024)
        zz = zz % 4
        own = jnp.concatenate([qg_v[zz, xh], gk_v[zz, xh]], axis=1)
        theirs = jnp.concatenate([g2[zz], k2[zz]], axis=1)
        return lax.dot_general(
            own, w_v[at, :], nt, preferred_element_type=F32
        ) + lax.dot_general(theirs, w2_v[at, :], nt, preferred_element_type=F32)

    def z_copy(stream, step):
        return send(
            z_tx.at[stream, step], z_rx.at[stream, step],
            zs.at[stream, step], zr.at[stream, step], around_z[stream // 2],
        )

    def z_step(step):
        for r in {0: (3, 1), 1: (2,), 2: (), 3: (0,)}[step]:
            far_copy(0, r).wait_recv()
            far_copy(1, r).wait_recv()
        for stream in (0, 2, 1, 3):
            target = z + 3 - step if stream < 2 else z + 1 + step
            term = row_term(target, stream * 1024)
            if step > 0:
                z_copy(stream, step - 1).wait_recv()
                term = term + z_rx[stream, step - 1].astype(F32)
            if step < 3:
                z_tx[stream, step] = term.astype(BF16)
                z_copy(stream, step).start()
            else:
                rows_out[:, stream * 1024 : (stream + 1) * 1024] = term.astype(BF16)

    def y_copy(stream, step):
        return send(
            y_tx.at[stream, step], y_rx.at[stream, step],
            ys.at[stream, step], yr.at[stream, step], around_y[stream],
        )

    def y_total(stream, step):
        target = y + 3 - step if stream == 0 else y + 1 + step
        total = weight_part(stream, target, c)
        core_copy(step * 2 + stream).wait_recv()
        total = total + c_rx[step * 2 + stream].astype(F32)
        if step > 0:
            y_copy(stream, step - 1).wait_recv()
            total = total + y_rx[stream, step - 1].astype(F32)
        return total

    def y_step(step):
        for stream in range(2):
            y_tx[stream, step] = y_total(stream, step).astype(BF16)
            y_copy(stream, step).start()

    z_step(0)
    y_step(0)
    z_step(1)
    y_step(1)
    y_step(2)
    z_step(2)
    sec_copy = send(s_tx, s_rx, ss, sr, partner)
    first, second = y_total(0, 3), y_total(1, 3)
    keep = jnp.where(sec == 0, first, second)
    s_tx[...] = jnp.where(sec == 0, second, first).astype(BF16)
    sec_copy.start()
    z_step(3)
    sec_copy.wait_recv()
    keep = (keep + s_rx[...].astype(F32)).T
    gq_out[...] = keep[:, :QW].astype(BF16)
    gk_out[...] = keep[:, QW:].astype(BF16)

    for copy in (key_send, sec_copy):
        copy.wait_send()
    for r in range(4):
        far_copy(0, r).wait_send()
        far_copy(1, r).wait_send()
    for i in range(8):
        core_copy(i).wait_send()
    for step in range(3):
        for stream in range(4):
            z_copy(stream, step).wait_send()
        for stream in range(2):
            y_copy(stream, step).wait_send()


def finish(qg, own, other, inputs, w_query, w_key, w2, rope):
    return pl.pallas_call(
        finish_kernel,
        out_shape=(
            jax.ShapeDtypeStruct((QB, D), BF16),
            jax.ShapeDtypeStruct((256, QW), BF16),
            jax.ShapeDtypeStruct((256, HD), BF16),
        ),
        in_specs=[ANY] * 8,
        out_specs=(VMEM, VMEM, VMEM),
        scratch_shapes=[
            pltpu.VMEM((ROWS, HD), F32),
            pltpu.VMEM((2, ROWS, HD), F32),
            pltpu.VMEM((ROWS, D), BF16),
            pltpu.VMEM((D, GW), BF16),
            pltpu.VMEM((D, GW), BF16),
            pltpu.VMEM((GW, ROWS), BF16),
            pltpu.VMEM((4, 2, QB, HD), BF16),
            pltpu.VMEM((ROWS, HD), BF16),
            pltpu.VMEM((4, QB, QW), BF16),
            pltpu.VMEM((4, QB, HD), BF16),
            pltpu.VMEM((4, 3, QB, 1024), BF16),
            pltpu.VMEM((4, 3, QB, 1024), BF16),
            pltpu.VMEM((8, GW, 256), BF16),
            pltpu.VMEM((8, GW, 256), BF16),
            pltpu.VMEM((2, 3, GW, 256), BF16),
            pltpu.VMEM((2, 3, GW, 256), BF16),
            pltpu.VMEM((GW, 256), BF16),
            pltpu.VMEM((GW, 256), BF16),
            pltpu.VMEM((4, 2, QB, QW), BF16),
            DMA((7,)),
            DMA, DMA,
            DMA((2, 4)), DMA((2, 4)),
            DMA((4, 3)), DMA((4, 3)),
            DMA((8,)), DMA((8,)),
            DMA((2, 3)), DMA((2, 3)),
            DMA, DMA,
        ],
        compiler_params=pltpu.CompilerParams(
            collective_id=2, has_side_effects=True, vmem_limit_bytes=63 * MIB
        ),
        name="finish",
    )(qg, own, other, inputs, w_query, w_key, w2, rope)


def close_kernel(rows, gq, gk, rows_out, gq_out, gk_out, rows_v, gq_v, gk_v, sems):
    triples = [(gk, gk_v, gk_out), (gq, gq_v, gq_out)]
    for part in range(4):
        at = pl.ds(part * 32, 32)
        triples.append((rows.at[at], rows_v.at[at], rows_out.at[0, at]))
    loads = [pltpu.make_async_copy(a, b, sems.at[0, i]) for i, (a, b, _) in enumerate(triples)]
    stores = [pltpu.make_async_copy(b, c, sems.at[1, i]) for i, (_, b, c) in enumerate(triples)]
    for load in loads:
        load.start()
    for load, store in zip(loads, stores):
        load.wait()
        store.start()
    for store in stores:
        store.wait()


def close(rows, grad_query, grad_key):
    held = [pltpu.VMEM(x.shape, x.dtype) for x in (rows, grad_query, grad_key)]
    return pl.pallas_call(
        close_kernel,
        out_shape=(
            jax.ShapeDtypeStruct((1,) + rows.shape, rows.dtype),
            jax.ShapeDtypeStruct(grad_query.shape, grad_query.dtype),
            jax.ShapeDtypeStruct(grad_key.shape, grad_key.dtype),
        ),
        in_specs=[ANY] * 3,
        out_specs=(ANY,) * 3,
        scratch_shapes=[*held, DMA((2, 6))],
        compiler_params=pltpu.CompilerParams(vmem_limit_bytes=63 * MIB),
        name="close",
    )(rows, grad_query, grad_key)


def shards(inputs, w_query, w_key, teacher_queries, teacher_keys, head_match, block_order):
    picked_k, picked_q, rope = pick(head_match, block_order, teacher_keys, teacher_queries)
    queries, keys, gotk, gotq, w2 = spread(picked_k, picked_q, inputs, w_query, w_key, rope)
    query_grads, own, other = attend(block_order, head_match, queries, keys, gotq, gotk, rope)
    rows, grad_query, grad_key = finish(
        query_grads.reshape(4, 2, QB, QW), own, other, inputs, w_query, w_key, w2, rope
    )
    return close(rows, grad_query, grad_key)


def solution(mesh):
    return jax.shard_map(
        shards,
        mesh=mesh,
        in_specs=(
            P("seq", "sec", None),
            P(None, "head"),
            P(None, "head"),
            P("seq", "head", "sec"),
            P("seq", "head", "sec"),
            P(),
            P(),
        ),
        out_specs=(
            P("seq", ("sec", "head"), None),
            P(("sec", "seq"), "head"),
            P(("sec", "seq"), "head"),
        ),
        check_vma=False,
    )
```

```python
import math

import jax
import jax.numpy as jnp
import numpy as np
from jax import lax
from jax.experimental import pallas as pl
from jax.experimental.pallas import tpu as pltpu
from jax.sharding import PartitionSpec as P

HD = 128
QB = 128
NBLK = 16
HALF_BLKS = 8
HEADS = 4
TH_SEC = 64
GROUPS = 8
ROWS = 1024
LEN = 2048
TROWS = 256
D = 4096
GW = 640
QW = 512
CK = 512
MIB = 1024 * 1024
LOWEST = -1e30

rope_base = 500000.0
grad_scale = 16.0
scale = 1.0 / math.sqrt(HD)
MESH = pl.DeviceIdType.MESH
ANY = pl.BlockSpec(memory_space=pl.ANY)
VMEM = pl.BlockSpec(memory_space=pltpu.VMEM)
SMEM = pl.BlockSpec(memory_space=pltpu.SMEM)
DMA = pltpu.SemaphoreType.DMA
F32 = jnp.float32
BF16 = jnp.bfloat16


def section_slots(match_ref, group, section):
    low, high = jnp.int32(TH_SEC - 1), jnp.int32(0)
    for i in range(HEADS):
        local = match_ref[group * HEADS + i] - section * TH_SEC
        inside = (local >= 0) & (local < TH_SEC)
        low = jnp.minimum(low, jnp.where(inside, local, TH_SEC - 1))
        high = jnp.maximum(high, jnp.where(inside, local, 0))
    return low, high


def pick_kernel(match_ref, tk_ref, tq_ref, k_out, q_out, k_v, q_v, in_sems, out_sems):
    sec = lax.axis_index("sec")
    copies = []
    for g in range(GROUPS):
        for j, local in enumerate(section_slots(match_ref, g, sec)):
            columns = pl.ds(pl.multiple_of(local * HD, HD), HD)
            for a, (src, held, dst) in enumerate(((tk_ref, k_v, k_out), (tq_ref, q_v, q_out))):
                place = held.at[g // 2, g % 2, j]
                load = pltpu.make_async_copy(src.at[0, :, columns], place, in_sems.at[a, g * 2 + j])
                load.start()
                store = pltpu.make_async_copy(
                    place, dst.at[g // 2, g % 2, j], out_sems.at[a, g * 2 + j]
                )
                copies.append((load, store))
    for load, store in copies:
        load.wait()
        store.start()
    for load, store in copies:
        store.wait()


def pick(match, teacher_keys, teacher_queries):
    shape = (4, 2, 2, TROWS, HD)
    return pl.pallas_call(
        pick_kernel,
        out_shape=(
            jax.ShapeDtypeStruct(shape, BF16),
            jax.ShapeDtypeStruct(shape, BF16),
        ),
        in_specs=[SMEM, ANY, ANY],
        out_specs=(ANY, ANY),
        scratch_shapes=[
            pltpu.VMEM(shape, BF16),
            pltpu.VMEM(shape, BF16),
            DMA((2, 16)),
            DMA((2, 16)),
        ],
        compiler_params=pltpu.CompilerParams(vmem_limit_bytes=63 * MIB),
        name="pick",
    )(match, teacher_keys, teacher_queries)


def spread_kernel(
    sk, sq, tok, wq, wk, order_ref, freqs,
    q_out, keys_out, gotk, gotq, w2, rope_v,
    tok_v, w_v, k_v, zk, zq,
    load_sem, own_sem, zs, zr, pks, pkr, cks, ckr, rks, rkr, qps, qpr, qxs, qxr,
    keys_s, keys_r, w1s, w1r, wys, wyr, wrs, wrr, wcs, wcr,
):
    sec, head, seq = lax.axis_index("sec"), lax.axis_index("head"), lax.axis_index("seq")
    z, xh = head // 2, head % 2
    y, c = seq // 2, seq % 2
    partner = {"sec": 1 - sec}
    cross = {"sec": 1 - sec, "head": z * 2 + 1 - xh}
    far = {"head": z * 2 + 1 - xh}
    core = {"seq": y * 2 + 1 - c}
    up = {"seq": ((y + 1) % 4) * 2 + c}
    down = {"seq": ((y + 3) % 4) * 2 + c}

    def depth(d):
        return {"head": ((z + d) % 4) * 2 + xh}

    def send(src, dst, ss, rs, where):
        return pltpu.make_async_remote_copy(
            src_ref=src, dst_ref=dst, send_sem=ss, recv_sem=rs, device_id=where, device_id_type=MESH
        )

    loads = [
        pltpu.make_async_copy(wq, w_v.at[:, pl.ds(0, QW)], load_sem.at[4]),
        pltpu.make_async_copy(wk, w_v.at[:, pl.ds(QW, HD)], load_sem.at[5]),
    ]
    for load in loads:
        load.start()

    def token_load(r):
        rows = pl.ds(pl.multiple_of(r * 256, 256), 256)
        return pltpu.make_async_copy(tok.at[0, rows], tok_v.at[rows], load_sem.at[r])

    for r in range(4):
        token_load(r).start()

    barrier = pltpu.get_barrier_semaphore()
    greet = [partner, cross, far, core, up, down, depth(1), depth(2), depth(3)]
    for where in greet:
        pl.semaphore_signal(barrier, inc=1, device_id=where, device_id_type=MESH)
    pl.semaphore_wait(barrier, len(greet))

    def along_z(a, d):
        src, dst = ((sk, zk), (sq, zq))[a]
        return send(
            src.at[(z + d) % 4], dst.at[d - 1], zs.at[a, d - 1], zr.at[a, d - 1], depth(d)
        )

    for d in (1, 3, 2):
        along_z(0, d).start()

    def krows(d, xhs):
        return pl.ds(pl.multiple_of((((z + 4 - d) % 4) * 2 + xhs) * TROWS, TROWS), TROWS)

    def qrows(d, xhs):
        return pl.ds(
            pl.multiple_of(((((z + 4 - d) % 4) * 2 + xhs) % 4) * TROWS, TROWS), TROWS
        )

    def held(d):
        return (sk.at[z], sq.at[z]) if d == 0 else (zk.at[d - 1], zq.at[d - 1])

    def along_x(d):
        kd, qd = held(d)
        half = ((z + 4 - d) % 4) // 2
        mine = gotk.at[sec, :, krows(d, xh)]
        mine_q = gotq.at[sec, :, qrows(d, xh)]
        return dict(
            ck=send(kd.at[1 - xh], mine, cks.at[d], ckr.at[d], cross),
            pk=send(kd.at[xh], mine, pks.at[d], pkr.at[d], partner),
            qx=send(
                qd.at[1 - xh], mine_q, qxs.at[d], qxr.at[d, sec],
                {"sec": half, "head": z * 2 + 1 - xh},
            ),
            qp=send(qd.at[xh], mine_q, qps.at[d], qpr.at[d], partner),
            lk=pltpu.make_async_copy(kd.at[xh], mine, own_sem.at[0, d]),
            lq=pltpu.make_async_copy(qd.at[xh], mine_q, own_sem.at[1, d]),
            half=half,
        )

    def start_keys(d):
        m = along_x(d)
        m["ck"].start()
        m["pk"].start()
        m["lk"].start()

    def start_queries(d):
        m = along_x(d)
        m["qx"].start()

        @pl.when(m["half"] != sec)
        def _():
            m["qp"].start()

        @pl.when(m["half"] == sec)
        def _():
            m["lq"].start()

    def relay(d):
        got = gotk.at[1 - sec, :, krows(d, 1 - xh)]
        return send(got, got, rks.at[d], rkr.at[d], partner)

    start_keys(0)
    start_queries(0)

    def rope_block(b, _):
        lane = lax.broadcasted_iota(jnp.int32, (QB, HD), 1)
        offset = lax.broadcasted_iota(jnp.int32, (QB, HD), 0)
        angles = (order_ref[sec * HALF_BLKS + b] * QB + offset).astype(F32) * freqs[...]
        at = pl.ds(pl.multiple_of(b * QB, QB), QB)
        sine = jnp.sin(angles)
        rope_v[0, at, :] = jnp.cos(angles)
        rope_v[1, at, :] = jnp.where(lane < HD // 2, -sine, sine)
        return 0

    for load in loads:
        load.wait()

    def piece(ref, yy, cc, j):
        start = ((yy % 4) * 2 + cc) * 512 + j * 256
        return ref.at[pl.ds(pl.multiple_of(start, 256), 256)]

    first = []

    def send_piece(j):
        copy = send(piece(w_v, y, c, j), piece(w2, y, c, j), w1s.at[j], w1r.at[j], cross)
        copy.start()
        first.append(copy)

    send_piece(0)
    lax.fori_loop(0, HALF_BLKS, rope_block, 0)

    def project(r, _):
        token_load(r).wait()
        rows = pl.ds(pl.multiple_of(r * 256, 256), 256)
        product = jnp.dot(tok_v[rows, :], w_v[...], preferred_element_type=F32)
        cosine, sine = rope_v[0, rows, :], rope_v[1, rows, :]
        for h in range(HEADS + 1):
            part = product[:, h * HD : (h + 1) * HD]
            part = (part * cosine + pltpu.roll(part, HD // 2, axis=1) * sine).astype(BF16)
            if h < HEADS:
                q_out[rows, h * HD : (h + 1) * HD] = part
            else:
                k_v[rows, :] = part
        return 0

    relays = []

    def wait_relay(d):
        got = gotk.at[1 - sec, :, krows(d, 1 - xh)]
        send(got, got, cks.at[d], ckr.at[d], cross).wait_recv()
        copy = relay(d)
        copy.start()
        relays.append(copy)

    wcopies = []

    def forward(src_y, j, sems, rsems, index, where):
        ref = piece(w2, src_y, c, j)
        copy = send(ref, ref, sems.at[index], rsems.at[index], where)
        copy.start()
        wcopies.append(copy)

    def wait_piece(src_y, cc, j, sem, rsem):
        ref = piece(w2, src_y, cc, j)
        send(ref, ref, sem, rsem, core).wait_recv()

    def spread_piece(j):
        wait_piece(y, c, j, w1s.at[j], w1r.at[j])
        forward(y, j, wys, wyr, j, up)
        forward(y, j, wys, wyr, 2 + j, down)
        forward(y, j, wcs, wcr, j, core)

    lax.fori_loop(0, 1, project, 0)
    for d in (1, 3, 2):
        along_z(1, d).start()
    lax.fori_loop(1, 2, project, 0)
    wait_relay(0)
    for d in (1, 3):
        along_z(0, d).wait_recv()
        start_keys(d)
    send_piece(1)
    lax.fori_loop(2, 3, project, 0)
    spread_piece(0)
    wait_relay(1)
    wait_relay(3)
    along_z(0, 2).wait_recv()
    start_keys(2)
    lax.fori_loop(3, 4, project, 0)
    key_rows = keys_out.at[pl.ds(pl.multiple_of(sec * ROWS, ROWS), ROWS)]
    key_send = send(k_v, key_rows, keys_s, keys_r, partner)
    key_send.start()
    key_own = pltpu.make_async_copy(k_v, key_rows, own_sem.at[2, 0])
    key_own.start()

    for d in (1, 3):
        along_z(1, d).wait_recv()
        start_queries(d)
    spread_piece(1)
    wait_piece(y + 3, c, 0, wys.at[0], wyr.at[0])
    forward(y + 3, 0, wrs, wrr, 0, up)
    forward(y + 3, 0, wcs, wcr, 2, core)
    wait_piece(y + 1, c, 1, wys.at[3], wyr.at[3])
    forward(y + 1, 1, wrs, wrr, 1, down)
    forward(y + 1, 1, wcs, wcr, 3, core)
    wait_relay(2)
    along_z(1, 2).wait_recv()
    start_queries(2)
    wait_piece(y + 3, c, 1, wys.at[1], wyr.at[1])
    forward(y + 3, 1, wcs, wcr, 4, core)
    wait_piece(y + 1, c, 0, wys.at[2], wyr.at[2])
    forward(y + 1, 0, wcs, wcr, 5, core)
    wait_piece(y + 2, c, 0, wrs.at[0], wrr.at[0])
    forward(y + 2, 0, wcs, wcr, 6, core)
    wait_piece(y + 2, c, 1, wrs.at[1], wrr.at[1])
    forward(y + 2, 1, wcs, wcr, 7, core)

    for index, (dy, j) in enumerate(((0, 0), (0, 1), (3, 0), (1, 1), (3, 1), (1, 0), (2, 0), (2, 1))):
        wait_piece(y + dy, 1 - c, j, wcs.at[index], wcr.at[index])
    other_rows = keys_out.at[pl.ds(pl.multiple_of((1 - sec) * ROWS, ROWS), ROWS)]
    send(k_v, other_rows, keys_s, keys_r, partner).wait_recv()
    for d in range(4):
        m = along_x(d)
        got = gotk.at[1 - sec, :, krows(d, xh)]
        send(got, got, pks.at[d], pkr.at[d], partner).wait_recv()
        got = gotk.at[sec, :, krows(d, 1 - xh)]
        send(got, got, rks.at[d], rkr.at[d], partner).wait_recv()

        @pl.when(m["half"] == sec)
        def _():
            got = gotq.at[1 - sec, :, qrows(d, xh)]
            send(got, got, qps.at[d], qpr.at[d], partner).wait_recv()
            for source in range(2):
                got = gotq.at[source, :, qrows(d, 1 - xh)]
                send(got, got, qxs.at[d], qxr.at[d, source], cross).wait_recv()
            m["lq"].wait()

        @pl.when(m["half"] != sec)
        def _():
            m["qp"].wait_send()

        m["lk"].wait()
        m["ck"].wait_send()
        m["pk"].wait_send()
        m["qx"].wait_send()
    key_own.wait()
    key_send.wait_send()
    for d in (1, 3, 2):
        for a in range(2):
            along_z(a, d).wait_send()
    for copy in first + relays + wcopies:
        copy.wait_send()


def spread(picked_k, picked_q, inputs, w_query, w_key, order):
    freqs = rope_base ** (-(np.arange(HD) % (HD // 2) * 2.0) / HD)
    freqs = jnp.asarray(freqs.astype(np.float32)[None])
    return pl.pallas_call(
        spread_kernel,
        out_shape=(
            jax.ShapeDtypeStruct((ROWS, QW), BF16),
            jax.ShapeDtypeStruct((LEN, HD), BF16),
            jax.ShapeDtypeStruct((2, 2, LEN, HD), BF16),
            jax.ShapeDtypeStruct((2, 2, ROWS, HD), BF16),
            jax.ShapeDtypeStruct((D, GW), BF16),
            jax.ShapeDtypeStruct((2, ROWS, HD), F32),
        ),
        in_specs=[ANY] * 5 + [SMEM, VMEM],
        out_specs=(VMEM, ANY, ANY, ANY, ANY, VMEM),
        scratch_shapes=[
            pltpu.VMEM((ROWS, D), BF16),
            pltpu.VMEM((D, GW), BF16),
            pltpu.VMEM((ROWS, HD), BF16),
            pltpu.VMEM((3, 2, 2, TROWS, HD), BF16),
            pltpu.VMEM((3, 2, 2, TROWS, HD), BF16),
            DMA((7,)),
            DMA((3, 4)),
            DMA((2, 3)), DMA((2, 3)),
            DMA((4,)), DMA((4,)),
            DMA((4,)), DMA((4,)),
            DMA((4,)), DMA((4,)),
            DMA((4,)), DMA((4,)),
            DMA((4,)), DMA((4, 2)),
            DMA, DMA,
            DMA((2,)), DMA((2,)),
            DMA((4,)), DMA((4,)),
            DMA((2,)), DMA((2,)),
            DMA((8,)), DMA((8,)),
        ],
        compiler_params=pltpu.CompilerParams(
            collective_id=1, has_side_effects=True, vmem_limit_bytes=63 * MIB
        ),
        name="spread",
    )(picked_k, picked_q, inputs, w_query, w_key, order, freqs)


def attend_kernel(
    order_ref, match_ref, q_ref, keys, gotq, gotk, rope,
    qg_ref, own_ref, other_ref,
    q_t, t_t, k_t, kp, tkp, tqv, st, ms, g_acc, dk, sems, qsems,
):
    sec, head = lax.axis_index("sec"), lax.axis_index("head")
    exponent = scale * math.log2(math.e)
    lows = [section_slots(match_ref, head, section)[0] for section in range(2)]
    places = []
    for i in range(HEADS):
        entry = match_ref[head * HEADS + i]
        section = entry // TH_SEC
        low = jnp.where(section == 0, lows[0], lows[1])
        slot = jnp.where(entry - section * TH_SEC == low, 0, 1)
        places.append((section, slot))
    copies = []
    for i, (section, slot) in enumerate(places):
        copies.append(pltpu.make_async_copy(gotq.at[section, slot], tqv.at[i], qsems.at[i]))
        copies[-1].start()
    for b in range(NBLK):
        to = pl.ds(pl.multiple_of(order_ref[b] * QB, QB), QB)
        at = pl.ds(b * QB, QB)
        copies.append(pltpu.make_async_copy(keys.at[at], kp.at[to], sems.at[4, b]))
        copies[-1].start()
        for i, (section, slot) in enumerate(places):
            copies.append(
                pltpu.make_async_copy(gotk.at[section, slot, at], tkp.at[i, to], sems.at[i, b])
            )
            copies[-1].start()
    dk[...] = jnp.zeros_like(dk)
    for copy in copies:
        copy.wait()

    for b in range(NBLK):
        k_t[:, b * QB : (b + 1) * QB] = kp[b * QB : (b + 1) * QB, :].T

    def one_block(qb, _):
        rows = pl.ds(pl.multiple_of(qb * QB, QB), QB)
        block = order_ref[sec * HALF_BLKS + qb]
        last = block // 4
        queries = jnp.concatenate(
            [q_ref[rows, i * HD : (i + 1) * HD] for i in range(HEADS)], axis=0
        )

        for i in range(HEADS):
            q_t[:, i * HD : (i + 1) * HD] = q_ref[rows, i * HD : (i + 1) * HD].T
            t_t[i] = tqv[i, rows, :].T

        def scores(chunk, carry, masked):
            at = pl.ds(pl.multiple_of(chunk * CK, CK), CK)
            tops, totals = [], []
            for unit in range(6):
                if unit < 2:
                    columns = slice(unit * 256, unit * 256 + 256)
                    part = jnp.dot(kp[at, :], q_t[:, columns], preferred_element_type=F32)
                else:
                    i = unit - 2
                    columns = slice(QW + i * HD, QW + (i + 1) * HD)
                    part = jnp.dot(tkp[i, at, :], t_t[i], preferred_element_type=F32)
                if masked:
                    key_at = lax.broadcasted_iota(jnp.int32, part.shape, 0) + chunk * CK
                    row_at = lax.broadcasted_iota(jnp.int32, part.shape, 1) % QB + block * QB
                    part = jnp.where(key_at <= row_at, part, LOWEST)
                part = part.reshape(CK // 8, 8, part.shape[1])
                before, total = carry[0][:, columns], carry[1][:, columns]
                top = jnp.maximum(before, jnp.max(part, axis=0))
                part = jnp.exp2((part - top[None]) * exponent)
                st[at, columns] = part.reshape(CK, part.shape[2])
                tops.append(top)
                totals.append(total * jnp.exp2((before - top) * exponent) + jnp.sum(part, axis=0))
            tops, totals = jnp.concatenate(tops, axis=1), jnp.concatenate(totals, axis=1)
            ms[chunk] = tops
            return tops, totals

        carry = (jnp.full((8, 2 * QW), LOWEST, F32), jnp.zeros((8, 2 * QW), F32))
        carry = lax.fori_loop(0, last, lambda chunk, t: scores(chunk, t, False), carry)
        tops, totals = scores(last, carry, True)
        top = jnp.max(tops, axis=0, keepdims=True)
        totals = totals * jnp.exp2((tops - top) * exponent)
        inverse = grad_scale / jnp.sum(totals, axis=0, keepdims=True)
        g_acc[...] = jnp.zeros_like(g_acc)

        def grads(chunk, _):
            at = pl.ds(pl.multiple_of(chunk * CK, CK), CK)
            factor = jnp.exp2((ms[chunk] - top) * exponent) * inverse
            both = st[at, :].reshape(CK // 8, 8, 2 * QW)
            g = both[:, :, :QW] * factor[None, :, :QW] - both[:, :, QW:] * factor[None, :, QW:]
            g = g.reshape(CK, QW).astype(BF16)
            dk[at, :] += jnp.dot(g, queries, preferred_element_type=F32)
            g_acc[...] += jnp.dot(k_t[:, at], g, preferred_element_type=F32)
            return 0

        lax.fori_loop(0, last + 1, grads, 0)
        cosine, sine = rope[0, rows, :], rope[1, rows, :]
        for i in range(HEADS):
            part = g_acc[:, i * QB : (i + 1) * QB].T * scale
            part = part * cosine - pltpu.roll(part, HD // 2, axis=1) * sine
            qg_ref[rows, i * HD : (i + 1) * HD] = part.astype(BF16)
        return 0

    lax.fori_loop(0, HALF_BLKS, one_block, 0)
    for b in range(HALF_BLKS):
        at = pl.ds(b * QB, QB)
        for half, ref in ((sec, own_ref), (1 - sec, other_ref)):
            block = order_ref[half * HALF_BLKS + b]
            part = dk[pl.ds(pl.multiple_of(block * QB, QB), QB), :] * scale
            ref[at, :] = part.astype(ref.dtype)


def attend(order, match, queries, keys, gotq, gotk, rope):
    return pl.pallas_call(
        attend_kernel,
        out_shape=(
            jax.ShapeDtypeStruct((ROWS, QW), BF16),
            jax.ShapeDtypeStruct((ROWS, HD), F32),
            jax.ShapeDtypeStruct((ROWS, HD), BF16),
        ),
        in_specs=[SMEM, SMEM, VMEM, ANY, ANY, ANY, VMEM],
        out_specs=(VMEM, VMEM, VMEM),
        scratch_shapes=[
            pltpu.VMEM((HD, QW), BF16),
            pltpu.VMEM((HEADS, HD, QB), BF16),
            pltpu.VMEM((HD, LEN), BF16),
            pltpu.VMEM((LEN, HD), BF16),
            pltpu.VMEM((HEADS, LEN, HD), BF16),
            pltpu.VMEM((HEADS, ROWS, HD), BF16),
            pltpu.VMEM((LEN, 2 * QW), F32),
            pltpu.VMEM((LEN // CK, 8, 2 * QW), F32),
            pltpu.VMEM((HD, QW), F32),
            pltpu.VMEM((LEN, HD), F32),
            DMA((HEADS + 1, NBLK)),
            DMA((HEADS,)),
        ],
        compiler_params=pltpu.CompilerParams(vmem_limit_bytes=63 * MIB),
        name="attend",
    )(order, match, queries, keys, gotq, gotk, rope)


def finish_kernel(
    qg, own, other, tok, wq, wk, w2, rope,
    rows_out, gq_out, gk_out,
    own_v, rope_v,
    tok_v, w_v, w2_v, gt, gk_v, key_rx, g2, k2, z_tx, z_rx, c_tx, c_rx, y_tx, y_rx, s_tx, s_rx, qg_v,
    load_sem, key_s, key_r, x_s, x_r, zs, zr, cs, cr, ys, yr, ss, sr,
):
    sec, head, seq = lax.axis_index("sec"), lax.axis_index("head"), lax.axis_index("seq")
    z, xh = head // 2, head % 2
    y, c = seq // 2, seq % 2
    partner = {"sec": 1 - sec}
    far = {"head": z * 2 + 1 - xh}
    core = {"seq": y * 2 + 1 - c}
    around_y = ({"seq": ((y + 1) % 4) * 2 + c}, {"seq": ((y + 3) % 4) * 2 + c})
    around_z = ({"head": ((z + 1) % 4) * 2 + xh}, {"head": ((z + 3) % 4) * 2 + xh})

    def send(src, dst, ss_, rs_, where):
        return pltpu.make_async_remote_copy(
            src_ref=src, dst_ref=dst, send_sem=ss_, recv_sem=rs_, device_id=where, device_id_type=MESH
        )

    loads = [
        pltpu.make_async_copy(qg, qg_v, load_sem.at[0]),
        pltpu.make_async_copy(tok.at[0], tok_v, load_sem.at[1]),
        pltpu.make_async_copy(wq, w_v.at[:, pl.ds(0, QW)], load_sem.at[2]),
        pltpu.make_async_copy(wk, w_v.at[:, pl.ds(QW, HD)], load_sem.at[3]),
        pltpu.make_async_copy(w2, w2_v, load_sem.at[4]),
    ]
    small = [
        pltpu.make_async_copy(own, own_v, load_sem.at[5]),
        pltpu.make_async_copy(rope, rope_v, load_sem.at[6]),
    ]
    for load in loads[:1] + small + loads[1:]:
        load.start()

    barrier = pltpu.get_barrier_semaphore()
    greet = [partner, far, core, *around_y, *around_z]
    for where in greet:
        pl.semaphore_signal(barrier, inc=1, device_id=where, device_id_type=MESH)
    pl.semaphore_wait(barrier, len(greet))

    key_send = send(other, key_rx, key_s, key_r, partner)
    key_send.start()

    def far_copy(a, r):
        zz = (z + r) % 4
        src, dst = ((qg, g2), (gk_v, k2))[a]
        return send(src.at[zz, 1 - xh], dst.at[zz], x_s.at[a, r], x_r.at[a, r], far)

    for r in (3, 1):
        far_copy(0, r).start()
    loads[0].wait()
    for b in range(HALF_BLKS):
        gt[0:QW, b * QB : (b + 1) * QB] = qg_v[b // 2, b % 2].T
    for load in small:
        load.wait()
    key_send.wait_recv()
    for b in range(HALF_BLKS):
        at = pl.ds(b * QB, QB)
        total = own_v[at, :] + key_rx[at, :].astype(F32)
        total = total * rope_v[0, at, :] - pltpu.roll(total, HD // 2, axis=1) * rope_v[1, at, :]
        total = total.astype(BF16)
        gk_v[b // 2, b % 2] = total
        gt[QW:GW, b * QB : (b + 1) * QB] = total.T
    for r in (3, 1, 2, 0):
        far_copy(1, r).start()
    for r in (2, 0):
        far_copy(0, r).start()

    def weight_part(s, yy, cc):
        start = (s * 8 + (yy % 4) * 2 + cc) * 256
        return jnp.dot(
            gt[...], tok_v[:, pl.ds(pl.multiple_of(start, 256), 256)], preferred_element_type=F32
        )

    def core_copy(i):
        return send(c_tx.at[i], c_rx.at[i], cs.at[i], cr.at[i], core)

    loads[1].wait()

    def to_core(i, _):
        s, step = i % 2, i // 2
        yy = jnp.where(s == 0, y + 3 - step, y + 1 + step) % 4
        c_tx[i] = weight_part(s, yy, 1 - c).astype(BF16)
        core_copy(i).start()
        return 0

    lax.fori_loop(0, 8, to_core, 0)
    for load in loads[2:]:
        load.wait()

    nt = (((1,), (1,)), ((), ()))

    def row_term(zz, column):
        at = pl.ds(column, 1024)
        zz = zz % 4
        own = jnp.concatenate([qg_v[zz, xh], gk_v[zz, xh]], axis=1)
        theirs = jnp.concatenate([g2[zz], k2[zz]], axis=1)
        return lax.dot_general(
            own, w_v[at, :], nt, preferred_element_type=F32
        ) + lax.dot_general(theirs, w2_v[at, :], nt, preferred_element_type=F32)

    def z_copy(stream, step):
        return send(
            z_tx.at[stream, step], z_rx.at[stream, step],
            zs.at[stream, step], zr.at[stream, step], around_z[stream // 2],
        )

    def z_step(step):
        for r in {0: (3, 1), 1: (2,), 2: (), 3: (0,)}[step]:
            far_copy(0, r).wait_recv()
            far_copy(1, r).wait_recv()
        for stream in (0, 2, 1, 3):
            target = z + 3 - step if stream < 2 else z + 1 + step
            term = row_term(target, stream * 1024)
            if step > 0:
                z_copy(stream, step - 1).wait_recv()
                term = term + z_rx[stream, step - 1].astype(F32)
            if step < 3:
                z_tx[stream, step] = term.astype(BF16)
                z_copy(stream, step).start()
            else:
                rows_out[:, stream * 1024 : (stream + 1) * 1024] = term.astype(BF16)

    def y_copy(stream, step):
        return send(
            y_tx.at[stream, step], y_rx.at[stream, step],
            ys.at[stream, step], yr.at[stream, step], around_y[stream],
        )

    def y_total(stream, step):
        target = y + 3 - step if stream == 0 else y + 1 + step
        total = weight_part(stream, target, c)
        core_copy(step * 2 + stream).wait_recv()
        total = total + c_rx[step * 2 + stream].astype(F32)
        if step > 0:
            y_copy(stream, step - 1).wait_recv()
            total = total + y_rx[stream, step - 1].astype(F32)
        return total

    def y_step(step):
        for stream in range(2):
            y_tx[stream, step] = y_total(stream, step).astype(BF16)
            y_copy(stream, step).start()

    z_step(0)
    y_step(0)
    z_step(1)
    y_step(1)
    y_step(2)
    z_step(2)
    sec_copy = send(s_tx, s_rx, ss, sr, partner)
    first, second = y_total(0, 3), y_total(1, 3)
    keep = jnp.where(sec == 0, first, second)
    s_tx[...] = jnp.where(sec == 0, second, first).astype(BF16)
    sec_copy.start()
    z_step(3)
    sec_copy.wait_recv()
    keep = (keep + s_rx[...].astype(F32)).T
    gq_out[...] = keep[:, :QW].astype(BF16)
    gk_out[...] = keep[:, QW:].astype(BF16)

    for copy in (key_send, sec_copy):
        copy.wait_send()
    for r in range(4):
        far_copy(0, r).wait_send()
        far_copy(1, r).wait_send()
    for i in range(8):
        core_copy(i).wait_send()
    for step in range(3):
        for stream in range(4):
            z_copy(stream, step).wait_send()
        for stream in range(2):
            y_copy(stream, step).wait_send()


def finish(qg, own, other, inputs, w_query, w_key, w2, rope):
    return pl.pallas_call(
        finish_kernel,
        out_shape=(
            jax.ShapeDtypeStruct((QB, D), BF16),
            jax.ShapeDtypeStruct((256, QW), BF16),
            jax.ShapeDtypeStruct((256, HD), BF16),
        ),
        in_specs=[ANY] * 8,
        out_specs=(VMEM, VMEM, VMEM),
        scratch_shapes=[
            pltpu.VMEM((ROWS, HD), F32),
            pltpu.VMEM((2, ROWS, HD), F32),
            pltpu.VMEM((ROWS, D), BF16),
            pltpu.VMEM((D, GW), BF16),
            pltpu.VMEM((D, GW), BF16),
            pltpu.VMEM((GW, ROWS), BF16),
            pltpu.VMEM((4, 2, QB, HD), BF16),
            pltpu.VMEM((ROWS, HD), BF16),
            pltpu.VMEM((4, QB, QW), BF16),
            pltpu.VMEM((4, QB, HD), BF16),
            pltpu.VMEM((4, 3, QB, 1024), BF16),
            pltpu.VMEM((4, 3, QB, 1024), BF16),
            pltpu.VMEM((8, GW, 256), BF16),
            pltpu.VMEM((8, GW, 256), BF16),
            pltpu.VMEM((2, 3, GW, 256), BF16),
            pltpu.VMEM((2, 3, GW, 256), BF16),
            pltpu.VMEM((GW, 256), BF16),
            pltpu.VMEM((GW, 256), BF16),
            pltpu.VMEM((4, 2, QB, QW), BF16),
            DMA((7,)),
            DMA, DMA,
            DMA((2, 4)), DMA((2, 4)),
            DMA((4, 3)), DMA((4, 3)),
            DMA((8,)), DMA((8,)),
            DMA((2, 3)), DMA((2, 3)),
            DMA, DMA,
        ],
        compiler_params=pltpu.CompilerParams(
            collective_id=2, has_side_effects=True, vmem_limit_bytes=63 * MIB
        ),
        name="finish",
    )(qg, own, other, inputs, w_query, w_key, w2, rope)


def close_kernel(rows, gq, gk, rows_out, gq_out, gk_out, rows_v, gq_v, gk_v, sems):
    triples = [(gk, gk_v, gk_out), (gq, gq_v, gq_out)]
    for part in range(4):
        at = pl.ds(part * 32, 32)
        triples.append((rows.at[at], rows_v.at[at], rows_out.at[0, at]))
    loads = [pltpu.make_async_copy(a, b, sems.at[0, i]) for i, (a, b, _) in enumerate(triples)]
    stores = [pltpu.make_async_copy(b, c, sems.at[1, i]) for i, (_, b, c) in enumerate(triples)]
    for load in loads:
        load.start()
    for load, store in zip(loads, stores):
        load.wait()
        store.start()
    for store in stores:
        store.wait()


def close(rows, grad_query, grad_key):
    held = [pltpu.VMEM(x.shape, x.dtype) for x in (rows, grad_query, grad_key)]
    return pl.pallas_call(
        close_kernel,
        out_shape=(
            jax.ShapeDtypeStruct((1,) + rows.shape, rows.dtype),
            jax.ShapeDtypeStruct(grad_query.shape, grad_query.dtype),
            jax.ShapeDtypeStruct(grad_key.shape, grad_key.dtype),
        ),
        in_specs=[ANY] * 3,
        out_specs=(ANY,) * 3,
        scratch_shapes=[*held, DMA((2, 6))],
        compiler_params=pltpu.CompilerParams(vmem_limit_bytes=63 * MIB),
        name="close",
    )(rows, grad_query, grad_key)


def shards(inputs, w_query, w_key, teacher_queries, teacher_keys, head_match, block_order):
    picked_k, picked_q = pick(head_match, teacher_keys, teacher_queries)
    queries, keys, gotk, gotq, w2, rope = spread(
        picked_k, picked_q, inputs, w_query, w_key, block_order
    )
    query_grads, own, other = attend(block_order, head_match, queries, keys, gotq, gotk, rope)
    rows, grad_query, grad_key = finish(
        query_grads.reshape(4, 2, QB, QW), own, other, inputs, w_query, w_key, w2, rope
    )
    return close(rows, grad_query, grad_key)


def solution(mesh):
    return jax.shard_map(
        shards,
        mesh=mesh,
        in_specs=(
            P("seq", "sec", None),
            P(None, "head"),
            P(None, "head"),
            P("seq", "head", "sec"),
            P("seq", "head", "sec"),
            P(),
            P(),
        ),
        out_specs=(
            P("seq", ("sec", "head"), None),
            P(("sec", "seq"), "head"),
            P(("sec", "seq"), "head"),
        ),
        check_vma=False,
    )
```

```python
import math

import jax
import jax.numpy as jnp
import numpy as np
from jax import lax
from jax.experimental import pallas as pl
from jax.experimental.pallas import tpu as pltpu
from jax.sharding import PartitionSpec as P

HD = 128
QB = 128
NBLK = 16
HALF_BLKS = 8
HEADS = 4
TH_SEC = 64
GROUPS = 8
ROWS = 1024
LEN = 2048
TROWS = 256
D = 4096
GW = 640
QW = 512
CK = 512
MIB = 1024 * 1024
LOWEST = -1e30

rope_base = 500000.0
grad_scale = 16.0
scale = 1.0 / math.sqrt(HD)
MESH = pl.DeviceIdType.MESH
ANY = pl.BlockSpec(memory_space=pl.ANY)
VMEM = pl.BlockSpec(memory_space=pltpu.VMEM)
SMEM = pl.BlockSpec(memory_space=pltpu.SMEM)
DMA = pltpu.SemaphoreType.DMA
F32 = jnp.float32
BF16 = jnp.bfloat16


def section_slots(match_ref, group, section):
    low, high = jnp.int32(TH_SEC - 1), jnp.int32(0)
    for i in range(HEADS):
        local = match_ref[group * HEADS + i] - section * TH_SEC
        inside = (local >= 0) & (local < TH_SEC)
        low = jnp.minimum(low, jnp.where(inside, local, TH_SEC - 1))
        high = jnp.maximum(high, jnp.where(inside, local, 0))
    return low, high


def pick_kernel(match_ref, tk_ref, tq_ref, k_out, q_out, k_v, q_v, in_sems, out_sems):
    sec = lax.axis_index("sec")
    copies = []
    for g in range(GROUPS):
        for j, local in enumerate(section_slots(match_ref, g, sec)):
            columns = pl.ds(pl.multiple_of(local * HD, HD), HD)
            for a, (src, held, dst) in enumerate(((tk_ref, k_v, k_out), (tq_ref, q_v, q_out))):
                place = held.at[g // 2, g % 2, j]
                load = pltpu.make_async_copy(src.at[0, :, columns], place, in_sems.at[a, g * 2 + j])
                load.start()
                store = pltpu.make_async_copy(
                    place, dst.at[g // 2, g % 2, j], out_sems.at[a, g * 2 + j]
                )
                copies.append((load, store))
    for load, store in copies:
        load.wait()
        store.start()
    for load, store in copies:
        store.wait()


def pick(match, teacher_keys, teacher_queries):
    shape = (4, 2, 2, TROWS, HD)
    return pl.pallas_call(
        pick_kernel,
        out_shape=(
            jax.ShapeDtypeStruct(shape, BF16),
            jax.ShapeDtypeStruct(shape, BF16),
        ),
        in_specs=[SMEM, ANY, ANY],
        out_specs=(ANY, ANY),
        scratch_shapes=[
            pltpu.VMEM(shape, BF16),
            pltpu.VMEM(shape, BF16),
            DMA((2, 16)),
            DMA((2, 16)),
        ],
        compiler_params=pltpu.CompilerParams(vmem_limit_bytes=63 * MIB),
        name="pick",
    )(match, teacher_keys, teacher_queries)


def spread_kernel(
    sk, sq, tok, wq, wk, order_ref, freqs,
    q_out, keys_out, gotk, gotq, w2, rope_v,
    tok_v, w_v, k_v, zk, zq,
    load_sem, own_sem, zs, zr, pks, pkr, cks, ckr, rks, rkr, qps, qpr, qxs, qxr,
    keys_s, keys_r, w1s, w1r, wys, wyr, wrs, wrr, wcs, wcr,
):
    sec, head, seq = lax.axis_index("sec"), lax.axis_index("head"), lax.axis_index("seq")
    z, xh = head // 2, head % 2
    y, c = seq // 2, seq % 2
    partner = {"sec": 1 - sec}
    cross = {"sec": 1 - sec, "head": z * 2 + 1 - xh}
    far = {"head": z * 2 + 1 - xh}
    core = {"seq": y * 2 + 1 - c}
    up = {"seq": ((y + 1) % 4) * 2 + c}
    down = {"seq": ((y + 3) % 4) * 2 + c}

    def depth(d):
        return {"head": ((z + d) % 4) * 2 + xh}

    def send(src, dst, ss, rs, where):
        return pltpu.make_async_remote_copy(
            src_ref=src, dst_ref=dst, send_sem=ss, recv_sem=rs, device_id=where, device_id_type=MESH
        )

    loads = [
        pltpu.make_async_copy(wq, w_v.at[:, pl.ds(0, QW)], load_sem.at[4]),
        pltpu.make_async_copy(wk, w_v.at[:, pl.ds(QW, HD)], load_sem.at[5]),
    ]
    for load in loads:
        load.start()

    def token_load(r):
        rows = pl.ds(pl.multiple_of(r * 256, 256), 256)
        return pltpu.make_async_copy(tok.at[0, rows], tok_v.at[rows], load_sem.at[r])

    for r in range(4):
        token_load(r).start()

    barrier = pltpu.get_barrier_semaphore()
    greet = [partner, cross, far, core, up, down, depth(1), depth(2), depth(3)]
    for where in greet:
        pl.semaphore_signal(barrier, inc=1, device_id=where, device_id_type=MESH)
    pl.semaphore_wait(barrier, len(greet))

    def along_z(a, d):
        src, dst = ((sk, zk), (sq, zq))[a]
        return send(
            src.at[(z + d) % 4], dst.at[d - 1], zs.at[a, d - 1], zr.at[a, d - 1], depth(d)
        )

    for d in (1, 3, 2):
        along_z(0, d).start()

    def krows(d, xhs):
        return pl.ds(pl.multiple_of((((z + 4 - d) % 4) * 2 + xhs) * TROWS, TROWS), TROWS)

    def qrows(d, xhs):
        return pl.ds(
            pl.multiple_of(((((z + 4 - d) % 4) * 2 + xhs) % 4) * TROWS, TROWS), TROWS
        )

    def held(d):
        return (sk.at[z], sq.at[z]) if d == 0 else (zk.at[d - 1], zq.at[d - 1])

    def along_x(d):
        kd, qd = held(d)
        half = ((z + 4 - d) % 4) // 2
        mine = gotk.at[sec, :, krows(d, xh)]
        mine_q = gotq.at[sec, :, qrows(d, xh)]
        return dict(
            ck=send(kd.at[1 - xh], mine, cks.at[d], ckr.at[d], cross),
            pk=send(kd.at[xh], mine, pks.at[d], pkr.at[d], partner),
            qx=send(
                qd.at[1 - xh], mine_q, qxs.at[d], qxr.at[d, sec],
                {"sec": half, "head": z * 2 + 1 - xh},
            ),
            qp=send(qd.at[xh], mine_q, qps.at[d], qpr.at[d], partner),
            lk=pltpu.make_async_copy(kd.at[xh], mine, own_sem.at[0, d]),
            lq=pltpu.make_async_copy(qd.at[xh], mine_q, own_sem.at[1, d]),
            half=half,
        )

    def start_keys(d):
        m = along_x(d)
        m["ck"].start()
        m["pk"].start()
        m["lk"].start()

    def start_queries(d):
        m = along_x(d)
        m["qx"].start()

        @pl.when(m["half"] != sec)
        def _():
            m["qp"].start()

        @pl.when(m["half"] == sec)
        def _():
            m["lq"].start()

    def relay(d):
        got = gotk.at[1 - sec, :, krows(d, 1 - xh)]
        return send(got, got, rks.at[d], rkr.at[d], partner)

    start_keys(0)
    start_queries(0)

    def rope_block(b, _):
        lane = lax.broadcasted_iota(jnp.int32, (QB, HD), 1)
        offset = lax.broadcasted_iota(jnp.int32, (QB, HD), 0)
        angles = (order_ref[sec * HALF_BLKS + b] * QB + offset).astype(F32) * freqs[...]
        at = pl.ds(pl.multiple_of(b * QB, QB), QB)
        sine = jnp.sin(angles)
        rope_v[0, at, :] = jnp.cos(angles)
        rope_v[1, at, :] = jnp.where(lane < HD // 2, -sine, sine)
        return 0

    for load in loads:
        load.wait()

    def piece(ref, yy, cc, j):
        start = ((yy % 4) * 2 + cc) * 512 + j * 256
        return ref.at[pl.ds(pl.multiple_of(start, 256), 256)]

    first = []

    def send_piece(j):
        copy = send(piece(w_v, y, c, j), piece(w2, y, c, j), w1s.at[j], w1r.at[j], cross)
        copy.start()
        first.append(copy)

    send_piece(0)
    lax.fori_loop(0, HALF_BLKS, rope_block, 0)

    def project(r, _):
        token_load(r).wait()
        rows = pl.ds(pl.multiple_of(r * 256, 256), 256)
        product = jnp.dot(tok_v[rows, :], w_v[...], preferred_element_type=F32)
        cosine, sine = rope_v[0, rows, :], rope_v[1, rows, :]
        for h in range(HEADS + 1):
            part = product[:, h * HD : (h + 1) * HD]
            part = (part * cosine + pltpu.roll(part, HD // 2, axis=1) * sine).astype(BF16)
            if h < HEADS:
                q_out[rows, h * HD : (h + 1) * HD] = part
            else:
                k_v[rows, :] = part
        return 0

    relays = []

    def wait_relay(d):
        got = gotk.at[1 - sec, :, krows(d, 1 - xh)]
        send(got, got, cks.at[d], ckr.at[d], cross).wait_recv()
        copy = relay(d)
        copy.start()
        relays.append(copy)

    wcopies = []

    def forward(src_y, j, sems, rsems, index, where):
        ref = piece(w2, src_y, c, j)
        copy = send(ref, ref, sems.at[index], rsems.at[index], where)
        copy.start()
        wcopies.append(copy)

    def wait_piece(src_y, cc, j, sem, rsem):
        ref = piece(w2, src_y, cc, j)
        send(ref, ref, sem, rsem, core).wait_recv()

    def spread_piece(j):
        wait_piece(y, c, j, w1s.at[j], w1r.at[j])
        forward(y, j, wys, wyr, j, up)
        forward(y, j, wys, wyr, 2 + j, down)
        forward(y, j, wcs, wcr, j, core)

    lax.fori_loop(0, 1, project, 0)
    for d in (1, 3, 2):
        along_z(1, d).start()
    lax.fori_loop(1, 2, project, 0)
    wait_relay(0)
    for d in (1, 3):
        along_z(0, d).wait_recv()
        start_keys(d)
    send_piece(1)
    lax.fori_loop(2, 3, project, 0)
    spread_piece(0)
    wait_relay(1)
    wait_relay(3)
    along_z(0, 2).wait_recv()
    start_keys(2)
    lax.fori_loop(3, 4, project, 0)
    key_rows = keys_out.at[pl.ds(pl.multiple_of(sec * ROWS, ROWS), ROWS)]
    key_send = send(k_v, key_rows, keys_s, keys_r, partner)
    key_send.start()
    key_own = pltpu.make_async_copy(k_v, key_rows, own_sem.at[2, 0])
    key_own.start()

    for d in (1, 3):
        along_z(1, d).wait_recv()
        start_queries(d)
    spread_piece(1)
    wait_piece(y + 3, c, 0, wys.at[0], wyr.at[0])
    forward(y + 3, 0, wrs, wrr, 0, up)
    forward(y + 3, 0, wcs, wcr, 2, core)
    wait_piece(y + 1, c, 1, wys.at[3], wyr.at[3])
    forward(y + 1, 1, wrs, wrr, 1, down)
    forward(y + 1, 1, wcs, wcr, 3, core)
    wait_relay(2)
    along_z(1, 2).wait_recv()
    start_queries(2)
    wait_piece(y + 3, c, 1, wys.at[1], wyr.at[1])
    forward(y + 3, 1, wcs, wcr, 4, core)
    wait_piece(y + 1, c, 0, wys.at[2], wyr.at[2])
    forward(y + 1, 0, wcs, wcr, 5, core)
    wait_piece(y + 2, c, 0, wrs.at[0], wrr.at[0])
    forward(y + 2, 0, wcs, wcr, 6, core)
    wait_piece(y + 2, c, 1, wrs.at[1], wrr.at[1])
    forward(y + 2, 1, wcs, wcr, 7, core)

    for index, (dy, j) in enumerate(((0, 0), (0, 1), (3, 0), (1, 1), (3, 1), (1, 0), (2, 0), (2, 1))):
        wait_piece(y + dy, 1 - c, j, wcs.at[index], wcr.at[index])
    other_rows = keys_out.at[pl.ds(pl.multiple_of((1 - sec) * ROWS, ROWS), ROWS)]
    send(k_v, other_rows, keys_s, keys_r, partner).wait_recv()
    for d in range(4):
        m = along_x(d)
        got = gotk.at[1 - sec, :, krows(d, xh)]
        send(got, got, pks.at[d], pkr.at[d], partner).wait_recv()
        got = gotk.at[sec, :, krows(d, 1 - xh)]
        send(got, got, rks.at[d], rkr.at[d], partner).wait_recv()

        @pl.when(m["half"] == sec)
        def _():
            got = gotq.at[1 - sec, :, qrows(d, xh)]
            send(got, got, qps.at[d], qpr.at[d], partner).wait_recv()
            for source in range(2):
                got = gotq.at[source, :, qrows(d, 1 - xh)]
                send(got, got, qxs.at[d], qxr.at[d, source], cross).wait_recv()
            m["lq"].wait()

        @pl.when(m["half"] != sec)
        def _():
            m["qp"].wait_send()

        m["lk"].wait()
        m["ck"].wait_send()
        m["pk"].wait_send()
        m["qx"].wait_send()
    key_own.wait()
    key_send.wait_send()
    for d in (1, 3, 2):
        for a in range(2):
            along_z(a, d).wait_send()
    for copy in first + relays + wcopies:
        copy.wait_send()


def spread(picked_k, picked_q, inputs, w_query, w_key, order):
    freqs = rope_base ** (-(np.arange(HD) % (HD // 2) * 2.0) / HD)
    freqs = jnp.asarray(freqs.astype(np.float32)[None])
    return pl.pallas_call(
        spread_kernel,
        out_shape=(
            jax.ShapeDtypeStruct((ROWS, QW), BF16),
            jax.ShapeDtypeStruct((LEN, HD), BF16),
            jax.ShapeDtypeStruct((2, 2, LEN, HD), BF16),
            jax.ShapeDtypeStruct((2, 2, ROWS, HD), BF16),
            jax.ShapeDtypeStruct((D, GW), BF16),
            jax.ShapeDtypeStruct((2, ROWS, HD), F32),
        ),
        in_specs=[ANY] * 5 + [SMEM, VMEM],
        out_specs=(VMEM, ANY, ANY, ANY, ANY, VMEM),
        scratch_shapes=[
            pltpu.VMEM((ROWS, D), BF16),
            pltpu.VMEM((D, GW), BF16),
            pltpu.VMEM((ROWS, HD), BF16),
            pltpu.VMEM((3, 2, 2, TROWS, HD), BF16),
            pltpu.VMEM((3, 2, 2, TROWS, HD), BF16),
            DMA((7,)),
            DMA((3, 4)),
            DMA((2, 3)), DMA((2, 3)),
            DMA((4,)), DMA((4,)),
            DMA((4,)), DMA((4,)),
            DMA((4,)), DMA((4,)),
            DMA((4,)), DMA((4,)),
            DMA((4,)), DMA((4, 2)),
            DMA, DMA,
            DMA((2,)), DMA((2,)),
            DMA((4,)), DMA((4,)),
            DMA((2,)), DMA((2,)),
            DMA((8,)), DMA((8,)),
        ],
        compiler_params=pltpu.CompilerParams(
            collective_id=1, has_side_effects=True, vmem_limit_bytes=63 * MIB
        ),
        name="spread",
    )(picked_k, picked_q, inputs, w_query, w_key, order, freqs)


def attend_kernel(
    order_ref, match_ref, q_in, keys, gotq, gotk, rope_in,
    qg_ref, own_ref, other_ref,
    q_ref, rope,
    q_t, t_t, k_t, kp, tkp, tqv, st, ms, g_acc, dk, sems, qsems,
):
    sec, head = lax.axis_index("sec"), lax.axis_index("head")
    exponent = scale * math.log2(math.e)
    lows = [section_slots(match_ref, head, section)[0] for section in range(2)]
    places = []
    for i in range(HEADS):
        entry = match_ref[head * HEADS + i]
        section = entry // TH_SEC
        low = jnp.where(section == 0, lows[0], lows[1])
        slot = jnp.where(entry - section * TH_SEC == low, 0, 1)
        places.append((section, slot))
    copies, key_copies = [], []
    for b in range(NBLK):
        to = pl.ds(pl.multiple_of(order_ref[b] * QB, QB), QB)
        at = pl.ds(b * QB, QB)
        key_copies.append(pltpu.make_async_copy(keys.at[at], kp.at[to], sems.at[4, b]))
        key_copies[-1].start()
    copies.append(pltpu.make_async_copy(q_in, q_ref, qsems.at[4]))
    copies[-1].start()
    copies.append(pltpu.make_async_copy(rope_in, rope, qsems.at[5]))
    copies[-1].start()
    for i, (section, slot) in enumerate(places):
        copies.append(pltpu.make_async_copy(gotq.at[section, slot], tqv.at[i], qsems.at[i]))
        copies[-1].start()
    for b in range(NBLK):
        to = pl.ds(pl.multiple_of(order_ref[b] * QB, QB), QB)
        at = pl.ds(b * QB, QB)
        for i, (section, slot) in enumerate(places):
            copies.append(
                pltpu.make_async_copy(gotk.at[section, slot, at], tkp.at[i, to], sems.at[i, b])
            )
            copies[-1].start()
    dk[...] = jnp.zeros_like(dk)
    for copy in key_copies:
        copy.wait()
    for b in range(NBLK):
        k_t[:, b * QB : (b + 1) * QB] = kp[b * QB : (b + 1) * QB, :].T
    for copy in copies:
        copy.wait()

    def one_block(qb, _):
        rows = pl.ds(pl.multiple_of(qb * QB, QB), QB)
        block = order_ref[sec * HALF_BLKS + qb]
        last = block // 4
        queries = jnp.concatenate(
            [q_ref[rows, i * HD : (i + 1) * HD] for i in range(HEADS)], axis=0
        )

        for i in range(HEADS):
            q_t[:, i * HD : (i + 1) * HD] = q_ref[rows, i * HD : (i + 1) * HD].T
            t_t[i] = tqv[i, rows, :].T

        def scores(chunk, carry, masked):
            at = pl.ds(pl.multiple_of(chunk * CK, CK), CK)
            tops, totals = [], []
            for unit in range(6):
                if unit < 2:
                    columns = slice(unit * 256, unit * 256 + 256)
                    part = jnp.dot(kp[at, :], q_t[:, columns], preferred_element_type=F32)
                else:
                    i = unit - 2
                    columns = slice(QW + i * HD, QW + (i + 1) * HD)
                    part = jnp.dot(tkp[i, at, :], t_t[i], preferred_element_type=F32)
                if masked:
                    key_at = lax.broadcasted_iota(jnp.int32, part.shape, 0) + chunk * CK
                    row_at = lax.broadcasted_iota(jnp.int32, part.shape, 1) % QB + block * QB
                    part = jnp.where(key_at <= row_at, part, LOWEST)
                part = part.reshape(CK // 8, 8, part.shape[1])
                before, total = carry[0][:, columns], carry[1][:, columns]
                top = jnp.maximum(before, jnp.max(part, axis=0))
                part = jnp.exp2((part - top[None]) * exponent)
                st[at, columns] = part.reshape(CK, part.shape[2])
                tops.append(top)
                totals.append(total * jnp.exp2((before - top) * exponent) + jnp.sum(part, axis=0))
            tops, totals = jnp.concatenate(tops, axis=1), jnp.concatenate(totals, axis=1)
            ms[chunk] = tops
            return tops, totals

        carry = (jnp.full((8, 2 * QW), LOWEST, F32), jnp.zeros((8, 2 * QW), F32))
        carry = lax.fori_loop(0, last, lambda chunk, t: scores(chunk, t, False), carry)
        tops, totals = scores(last, carry, True)
        top = jnp.max(tops, axis=0, keepdims=True)
        totals = totals * jnp.exp2((tops - top) * exponent)
        inverse = grad_scale / jnp.sum(totals, axis=0, keepdims=True)
        g_acc[...] = jnp.zeros_like(g_acc)

        def grads(chunk, _):
            at = pl.ds(pl.multiple_of(chunk * CK, CK), CK)
            factor = jnp.exp2((ms[chunk] - top) * exponent) * inverse
            key_part = None
            for pair in range(2):
                student = slice(pair * 256, pair * 256 + 256)
                teacher = slice(QW + pair * 256, QW + pair * 256 + 256)
                p_s = st[at, student].reshape(CK // 8, 8, 256) * factor[None, :, student]
                p_t = st[at, teacher].reshape(CK // 8, 8, 256) * factor[None, :, teacher]
                g = (p_s - p_t).reshape(CK, 256).astype(BF16)
                term = jnp.dot(g, queries[student], preferred_element_type=F32)
                key_part = term if key_part is None else key_part + term
                g_acc[:, student] += jnp.dot(k_t[:, at], g, preferred_element_type=F32)
            dk[at, :] += key_part
            return 0

        lax.fori_loop(0, last + 1, grads, 0)
        cosine, sine = rope[0, rows, :], rope[1, rows, :]
        for i in range(HEADS):
            part = g_acc[:, i * QB : (i + 1) * QB].T * scale
            part = part * cosine - pltpu.roll(part, HD // 2, axis=1) * sine
            qg_ref[rows, i * HD : (i + 1) * HD] = part.astype(BF16)
        return 0

    lax.fori_loop(0, HALF_BLKS, one_block, 0)
    for b in range(HALF_BLKS):
        at = pl.ds(b * QB, QB)
        for half, ref in ((sec, own_ref), (1 - sec, other_ref)):
            block = order_ref[half * HALF_BLKS + b]
            part = dk[pl.ds(pl.multiple_of(block * QB, QB), QB), :] * scale
            ref[at, :] = part.astype(ref.dtype)


def attend(order, match, queries, keys, gotq, gotk, rope):
    return pl.pallas_call(
        attend_kernel,
        out_shape=(
            jax.ShapeDtypeStruct((ROWS, QW), BF16),
            jax.ShapeDtypeStruct((ROWS, HD), F32),
            jax.ShapeDtypeStruct((ROWS, HD), BF16),
        ),
        in_specs=[SMEM, SMEM, ANY, ANY, ANY, ANY, ANY],
        out_specs=(VMEM, VMEM, VMEM),
        scratch_shapes=[
            pltpu.VMEM((ROWS, QW), BF16),
            pltpu.VMEM((2, ROWS, HD), F32),
            pltpu.VMEM((HD, QW), BF16),
            pltpu.VMEM((HEADS, HD, QB), BF16),
            pltpu.VMEM((HD, LEN), BF16),
            pltpu.VMEM((LEN, HD), BF16),
            pltpu.VMEM((HEADS, LEN, HD), BF16),
            pltpu.VMEM((HEADS, ROWS, HD), BF16),
            pltpu.VMEM((LEN, 2 * QW), F32),
            pltpu.VMEM((LEN // CK, 8, 2 * QW), F32),
            pltpu.VMEM((HD, QW), F32),
            pltpu.VMEM((LEN, HD), F32),
            DMA((HEADS + 1, NBLK)),
            DMA((HEADS + 2,)),
        ],
        compiler_params=pltpu.CompilerParams(vmem_limit_bytes=63 * MIB),
        name="attend",
    )(order, match, queries, keys, gotq, gotk, rope)


def finish_kernel(
    qg, own, other, tok, wq, wk, w2, rope,
    rows_out, gq_out, gk_out,
    own_v, rope_v,
    tok_v, w_v, w2_v, gt, gk_v, key_rx, g2, k2, z_tx, z_rx, c_tx, c_rx, y_tx, y_rx, s_tx, s_rx, qg_v,
    load_sem, key_s, key_r, x_s, x_r, zs, zr, cs, cr, ys, yr, ss, sr,
):
    sec, head, seq = lax.axis_index("sec"), lax.axis_index("head"), lax.axis_index("seq")
    z, xh = head // 2, head % 2
    y, c = seq // 2, seq % 2
    partner = {"sec": 1 - sec}
    far = {"head": z * 2 + 1 - xh}
    core = {"seq": y * 2 + 1 - c}
    around_y = ({"seq": ((y + 1) % 4) * 2 + c}, {"seq": ((y + 3) % 4) * 2 + c})
    around_z = ({"head": ((z + 1) % 4) * 2 + xh}, {"head": ((z + 3) % 4) * 2 + xh})

    def send(src, dst, ss_, rs_, where):
        return pltpu.make_async_remote_copy(
            src_ref=src, dst_ref=dst, send_sem=ss_, recv_sem=rs_, device_id=where, device_id_type=MESH
        )

    loads = [
        pltpu.make_async_copy(qg, qg_v, load_sem.at[0]),
        pltpu.make_async_copy(tok.at[0], tok_v, load_sem.at[1]),
        pltpu.make_async_copy(wq, w_v.at[:, pl.ds(0, QW)], load_sem.at[2]),
        pltpu.make_async_copy(wk, w_v.at[:, pl.ds(QW, HD)], load_sem.at[3]),
        pltpu.make_async_copy(w2, w2_v, load_sem.at[4]),
    ]
    small = [
        pltpu.make_async_copy(own, own_v, load_sem.at[5]),
        pltpu.make_async_copy(rope, rope_v, load_sem.at[6]),
    ]
    for load in loads[:1] + small + loads[1:]:
        load.start()

    barrier = pltpu.get_barrier_semaphore()
    greet = [partner, far, core, *around_y, *around_z]
    for where in greet:
        pl.semaphore_signal(barrier, inc=1, device_id=where, device_id_type=MESH)
    pl.semaphore_wait(barrier, len(greet))

    key_send = send(other, key_rx, key_s, key_r, partner)
    key_send.start()

    def far_copy(a, r):
        zz = (z + r) % 4
        src, dst = ((qg, g2), (gk_v, k2))[a]
        return send(src.at[zz, 1 - xh], dst.at[zz], x_s.at[a, r], x_r.at[a, r], far)

    for r in (3, 1):
        far_copy(0, r).start()
    loads[0].wait()
    for b in range(HALF_BLKS):
        gt[0:QW, b * QB : (b + 1) * QB] = qg_v[b // 2, b % 2].T
    for load in small:
        load.wait()
    key_send.wait_recv()
    for b in range(HALF_BLKS):
        at = pl.ds(b * QB, QB)
        total = own_v[at, :] + key_rx[at, :].astype(F32)
        total = total * rope_v[0, at, :] - pltpu.roll(total, HD // 2, axis=1) * rope_v[1, at, :]
        total = total.astype(BF16)
        gk_v[b // 2, b % 2] = total
        gt[QW:GW, b * QB : (b + 1) * QB] = total.T
    for r in (3, 1, 2, 0):
        far_copy(1, r).start()
    for r in (2, 0):
        far_copy(0, r).start()

    def weight_part(s, yy, cc):
        start = (s * 8 + (yy % 4) * 2 + cc) * 256
        return jnp.dot(
            gt[...], tok_v[:, pl.ds(pl.multiple_of(start, 256), 256)], preferred_element_type=F32
        )

    def core_copy(i):
        return send(c_tx.at[i], c_rx.at[i], cs.at[i], cr.at[i], core)

    loads[1].wait()

    def to_core(i, _):
        s, step = i % 2, i // 2
        yy = jnp.where(s == 0, y + 3 - step, y + 1 + step) % 4
        c_tx[i] = weight_part(s, yy, 1 - c).astype(BF16)
        core_copy(i).start()
        return 0

    lax.fori_loop(0, 8, to_core, 0)
    for load in loads[2:]:
        load.wait()

    nt = (((1,), (1,)), ((), ()))

    def row_term(zz, column):
        at = pl.ds(column, 1024)
        zz = zz % 4
        own = jnp.concatenate([qg_v[zz, xh], gk_v[zz, xh]], axis=1)
        theirs = jnp.concatenate([g2[zz], k2[zz]], axis=1)
        return lax.dot_general(
            own, w_v[at, :], nt, preferred_element_type=F32
        ) + lax.dot_general(theirs, w2_v[at, :], nt, preferred_element_type=F32)

    def z_copy(stream, step):
        return send(
            z_tx.at[stream, step], z_rx.at[stream, step],
            zs.at[stream, step], zr.at[stream, step], around_z[stream // 2],
        )

    def z_step(step):
        for r in {0: (3, 1), 1: (2,), 2: (), 3: (0,)}[step]:
            far_copy(0, r).wait_recv()
            far_copy(1, r).wait_recv()
        for stream in (0, 2, 1, 3):
            target = z + 3 - step if stream < 2 else z + 1 + step
            term = row_term(target, stream * 1024)
            if step > 0:
                z_copy(stream, step - 1).wait_recv()
                term = term + z_rx[stream, step - 1].astype(F32)
            if step < 3:
                z_tx[stream, step] = term.astype(BF16)
                z_copy(stream, step).start()
            else:
                rows_out[:, stream * 1024 : (stream + 1) * 1024] = term.astype(BF16)

    def y_copy(stream, step):
        return send(
            y_tx.at[stream, step], y_rx.at[stream, step],
            ys.at[stream, step], yr.at[stream, step], around_y[stream],
        )

    def y_total(stream, step):
        target = y + 3 - step if stream == 0 else y + 1 + step
        total = weight_part(stream, target, c)
        core_copy(step * 2 + stream).wait_recv()
        total = total + c_rx[step * 2 + stream].astype(F32)
        if step > 0:
            y_copy(stream, step - 1).wait_recv()
            total = total + y_rx[stream, step - 1].astype(F32)
        return total

    def y_step(step):
        for stream in range(2):
            y_tx[stream, step] = y_total(stream, step).astype(BF16)
            y_copy(stream, step).start()

    z_step(0)
    y_step(0)
    z_step(1)
    y_step(1)
    y_step(2)
    z_step(2)
    sec_copy = send(s_tx, s_rx, ss, sr, partner)
    first, second = y_total(0, 3), y_total(1, 3)
    keep = jnp.where(sec == 0, first, second)
    s_tx[...] = jnp.where(sec == 0, second, first).astype(BF16)
    sec_copy.start()
    z_step(3)
    sec_copy.wait_recv()
    keep = (keep + s_rx[...].astype(F32)).T
    gq_out[...] = keep[:, :QW].astype(BF16)
    gk_out[...] = keep[:, QW:].astype(BF16)

    for copy in (key_send, sec_copy):
        copy.wait_send()
    for r in range(4):
        far_copy(0, r).wait_send()
        far_copy(1, r).wait_send()
    for i in range(8):
        core_copy(i).wait_send()
    for step in range(3):
        for stream in range(4):
            z_copy(stream, step).wait_send()
        for stream in range(2):
            y_copy(stream, step).wait_send()


def finish(qg, own, other, inputs, w_query, w_key, w2, rope):
    return pl.pallas_call(
        finish_kernel,
        out_shape=(
            jax.ShapeDtypeStruct((QB, D), BF16),
            jax.ShapeDtypeStruct((256, QW), BF16),
            jax.ShapeDtypeStruct((256, HD), BF16),
        ),
        in_specs=[ANY] * 8,
        out_specs=(VMEM, VMEM, VMEM),
        scratch_shapes=[
            pltpu.VMEM((ROWS, HD), F32),
            pltpu.VMEM((2, ROWS, HD), F32),
            pltpu.VMEM((ROWS, D), BF16),
            pltpu.VMEM((D, GW), BF16),
            pltpu.VMEM((D, GW), BF16),
            pltpu.VMEM((GW, ROWS), BF16),
            pltpu.VMEM((4, 2, QB, HD), BF16),
            pltpu.VMEM((ROWS, HD), BF16),
            pltpu.VMEM((4, QB, QW), BF16),
            pltpu.VMEM((4, QB, HD), BF16),
            pltpu.VMEM((4, 3, QB, 1024), BF16),
            pltpu.VMEM((4, 3, QB, 1024), BF16),
            pltpu.VMEM((8, GW, 256), BF16),
            pltpu.VMEM((8, GW, 256), BF16),
            pltpu.VMEM((2, 3, GW, 256), BF16),
            pltpu.VMEM((2, 3, GW, 256), BF16),
            pltpu.VMEM((GW, 256), BF16),
            pltpu.VMEM((GW, 256), BF16),
            pltpu.VMEM((4, 2, QB, QW), BF16),
            DMA((7,)),
            DMA, DMA,
            DMA((2, 4)), DMA((2, 4)),
            DMA((4, 3)), DMA((4, 3)),
            DMA((8,)), DMA((8,)),
            DMA((2, 3)), DMA((2, 3)),
            DMA, DMA,
        ],
        compiler_params=pltpu.CompilerParams(
            collective_id=2, has_side_effects=True, vmem_limit_bytes=63 * MIB
        ),
        name="finish",
    )(qg, own, other, inputs, w_query, w_key, w2, rope)


def close_kernel(rows, gq, gk, rows_out, gq_out, gk_out, rows_v, gq_v, gk_v, sems):
    triples = [(gk, gk_v, gk_out), (gq, gq_v, gq_out)]
    for part in range(4):
        at = pl.ds(part * 32, 32)
        triples.append((rows.at[at], rows_v.at[at], rows_out.at[0, at]))
    loads = [pltpu.make_async_copy(a, b, sems.at[0, i]) for i, (a, b, _) in enumerate(triples)]
    stores = [pltpu.make_async_copy(b, c, sems.at[1, i]) for i, (_, b, c) in enumerate(triples)]
    for load in loads:
        load.start()
    for load, store in zip(loads, stores):
        load.wait()
        store.start()
    for store in stores:
        store.wait()


def close(rows, grad_query, grad_key):
    held = [pltpu.VMEM(x.shape, x.dtype) for x in (rows, grad_query, grad_key)]
    return pl.pallas_call(
        close_kernel,
        out_shape=(
            jax.ShapeDtypeStruct((1,) + rows.shape, rows.dtype),
            jax.ShapeDtypeStruct(grad_query.shape, grad_query.dtype),
            jax.ShapeDtypeStruct(grad_key.shape, grad_key.dtype),
        ),
        in_specs=[ANY] * 3,
        out_specs=(ANY,) * 3,
        scratch_shapes=[*held, DMA((2, 6))],
        compiler_params=pltpu.CompilerParams(vmem_limit_bytes=63 * MIB),
        name="close",
    )(rows, grad_query, grad_key)


def shards(inputs, w_query, w_key, teacher_queries, teacher_keys, head_match, block_order):
    picked_k, picked_q = pick(head_match, teacher_keys, teacher_queries)
    queries, keys, gotk, gotq, w2, rope = spread(
        picked_k, picked_q, inputs, w_query, w_key, block_order
    )
    query_grads, own, other = attend(block_order, head_match, queries, keys, gotq, gotk, rope)
    rows, grad_query, grad_key = finish(
        query_grads.reshape(4, 2, QB, QW), own, other, inputs, w_query, w_key, w2, rope
    )
    return close(rows, grad_query, grad_key)


def solution(mesh):
    return jax.shard_map(
        shards,
        mesh=mesh,
        in_specs=(
            P("seq", "sec", None),
            P(None, "head"),
            P(None, "head"),
            P("seq", "head", "sec"),
            P("seq", "head", "sec"),
            P(),
            P(),
        ),
        out_specs=(
            P("seq", ("sec", "head"), None),
            P(("sec", "seq"), "head"),
            P(("sec", "seq"), "head"),
        ),
        check_vma=False,
    )
```
